512 devices in a mesh: dp: 16 (over z), axial: 32 (over x, y, core).
Axes of the slice: x: 4, y: 4, z: 16, core: 2. Of those that a mesh axis runs over, the one named last changes fastest.
Arguments:
- pair: bfloat16 [16, 256, 256, 128], P('dp', 'axial'), may hold values from -6 to 6
- cotangent: bfloat16 [16, 256, 256, 128], P('dp', 'axial'), may hold values from -6 to 6
- lengths: int32 [16], P('dp'), may hold values from 1 to 256, 2560 in all
- outgo_norm: float32 [128], replicated, may hold values from 0.1 to 1.9
- outgo_proj: float32 [128, 640], replicated, may hold values from -0.5 to 0.5
- outgo_gain: float32 [128], replicated, may hold values from 0.1 to 1.9
- outgo_final: float32 [128, 128], replicated, may hold values from -0.5 to 0.5
- incom_norm: float32 [128], replicated, may hold values from 0.1 to 1.9
- incom_proj: float32 [128, 640], replicated, may hold values from -0.5 to 0.5
- incom_gain: float32 [128], replicated, may hold values from 0.1 to 1.9
- incom_final: float32 [128, 128], replicated, may hold values from -0.5 to 0.5
Outputs:
- grad_pair: float32 [16, 256, 256, 128], P('dp', 'axial')
- grad_outgo_norm: float32 [128], replicated
- grad_outgo_proj: float32 [128, 640], replicated
- grad_outgo_gain: float32 [128], replicated
- grad_outgo_final: float32 [128, 128], replicated
- grad_incom_norm: float32 [128], replicated
- grad_incom_proj: float32 [128, 640], replicated
- grad_incom_gain: float32 [128], replicated
- grad_incom_final: float32 [128, 128], replicated
The draws below stay inside these ranges and needn't reach their ends.
Inputs may be any that keep to these rules, and one draw needn't show every extreme that they name: lengths[c] is the crop length of complex c; some complex has exactly 256 tokens.
All inputs are finite; a program needn't handle non-finite values. No bound on the sum of `lengths` on one device may be relied on, other than what follows from the above.
Results may differ from the reference program's by a relative error of at most 0.03.
Values may be sent and summed in bfloat16 or wider, within the bound.
A program may use at most 128 MiB of HBM per device.

```python
import math
import jax
import jax.numpy as jnp
import numpy as np
from jax import lax

C = 128
H = 128
TOK = 256
N_DP = 16


def steps_of(own_key, shape, split, low, top_value):
    def one(dim, blocks):
        heights = jax.random.uniform(jax.random.fold_in(jax.random.fold_in(own_key, 6), dim), (blocks,), jnp.float32, low / len(split), top_value / len(split))
        return jnp.repeat(jnp.exp(heights), shape[dim] // blocks).reshape((-1,) + (1,) * (len(shape) - dim - 1))

    factor_of = one(*split[0])
    for cut in split[1:]:
        factor_of = factor_of * one(*cut)
    return factor_of


def split_up(amount, total, bound, lean):
    loads = [(1 << 20) // math.isqrt(rank ** lean) + 1 for rank in range(2, amount + 1)]
    surplus, counts = total - bound - (amount - 1), [1] * (amount - 1)
    while surplus > 0:
        free = [i for i in range(amount - 1) if counts[i] < bound]
        mass, budget = sum([loads[i] for i in free]), surplus
        for i in free:
            extra = min(bound - counts[i], max(1, budget * loads[i] // mass), surplus)
            counts[i] = counts[i] + extra
            surplus = surplus - extra
    return np.array([bound] + counts)


def uneven(key, count, total, reach, skew):
    if count == 2:
        one = jax.random.randint(key, (), max(1, total - reach), min(reach, total - 1) + 1)
        return jnp.stack([one, total - one])
    sizes = jnp.asarray(split_up(count, total, reach, skew), jnp.int32)
    twos = (count - 1) // 2
    source_of, sink = sizes[1:1 + 2 * twos:2], sizes[2:2 + 2 * twos:2]
    slack = jnp.minimum(source_of - 1, reach - sink)
    passed = jax.random.randint(jax.random.fold_in(key, 1), (twos,), 0, 1 << 20) % (slack + 1)
    sizes = sizes.at[1:1 + 2 * twos:2].set(source_of - passed).at[2:2 + 2 * twos:2].set(sink + passed)
    return sizes[jax.random.permutation(jax.random.fold_in(key, 2), count)]


def noise(rng, dims, deviation, most, pieces=(), kind=jnp.bfloat16):
    entries = deviation * jax.random.normal(rng, dims, jnp.float32)
    if pieces:
        entries = entries * steps_of(rng, dims, pieces, -0.22, 0.18)
    return jnp.clip(entries, -most, most).astype(kind)


def setup_inputs(seed: int = 0) -> dict:
    arg_keys = jax.random.split(jax.random.key(seed), 12)
    return {
        "pair": noise(arg_keys[0], (N_DP, TOK, TOK, C), 1.0, 6.0, ((0, 16), (1, 32))),
        "cotangent": noise(arg_keys[1], (N_DP, TOK, TOK, C), 1.0, 6.0, ((0, 16), (1, 32))),
        "lengths": uneven(arg_keys[2], N_DP, N_DP * TOK * 5 // 8, TOK, 0).astype(jnp.int32),
        "outgo_norm": jnp.clip(1.0 + 0.18 * jax.random.normal(arg_keys[3], (C,), jnp.float32), 0.1, 1.9),
        "outgo_proj": noise(arg_keys[4], (C, 4 * H + C), C ** -0.5, 0.5, (), jnp.float32),
        "outgo_gain": jnp.clip(1.0 + 0.18 * jax.random.normal(arg_keys[5], (H,), jnp.float32), 0.1, 1.9),
        "outgo_final": noise(arg_keys[6], (H, C), H ** -0.5, 0.5, (), jnp.float32),
        "incom_norm": jnp.clip(1.0 + 0.18 * jax.random.normal(arg_keys[7], (C,), jnp.float32), 0.1, 1.9),
        "incom_proj": noise(arg_keys[8], (C, 4 * H + C), C ** -0.5, 0.5, (), jnp.float32),
        "incom_gain": jnp.clip(1.0 + 0.18 * jax.random.normal(arg_keys[9], (H,), jnp.float32), 0.1, 1.9),
        "incom_final": noise(arg_keys[10], (H, C), H ** -0.5, 0.5, (), jnp.float32),
    }


EPSILON = 1e-05

def rounded(inputs):
    return lax.optimization_barrier(inputs.astype(jnp.bfloat16)).astype(jnp.float32)

def layer_norm(inputs, factor):
    average = lax.optimization_barrier(jnp.mean(inputs, axis=-1, keepdims=True))
    centered = inputs - average
    spread = lax.optimization_barrier(jnp.mean(centered * centered, axis=-1, keepdims=True))
    return centered * lax.rsqrt(spread + EPSILON) * factor

def gating(mixture, pair_mask, hidden):
    left_part = mixture[:, :hidden] * jax.nn.sigmoid(mixture[:, 2 * hidden:3 * hidden]) * pair_mask
    right_part = mixture[:, hidden:2 * hidden] * jax.nn.sigmoid(mixture[:, 3 * hidden:4 * hidden]) * pair_mask
    gate_part = jax.nn.sigmoid(mixture[:, 4 * hidden:])
    return (left_part, right_part, gate_part)

def entry(flat_pair, norm_gain, projection, pair_mask, hidden):
    normed = layer_norm(flat_pair, norm_gain).astype(jnp.bfloat16)
    mixture = jnp.dot(normed, projection.astype(jnp.bfloat16), preferred_element_type=jnp.float32)
    left_part, right_part, gate_part = gating(mixture, pair_mask, hidden)
    return (normed, mixture, left_part, right_part, gate_part)

def entry_back(flat_pair, norm_gain, projection, pair_mask, hidden, normed, mixture, grad_left, grad_right, grad_gate):
    unused, pull_gate = jax.vjp(lambda inner_mix: gating(inner_mix, pair_mask, hidden), mixture)
    grad_mixture = pull_gate((grad_left, grad_right, grad_gate))[0].astype(jnp.bfloat16)
    grad_projection = jnp.dot(normed.T, grad_mixture, preferred_element_type=jnp.float32)
    grad_normed = jnp.dot(grad_mixture, projection.astype(jnp.bfloat16).T, preferred_element_type=jnp.float32)
    unused, pull_norm = jax.vjp(layer_norm, flat_pair, norm_gain)
    grad_flat, grad_gain = pull_norm(grad_normed)
    return (grad_flat, grad_gain, grad_projection)

def leave(inner_sum, gate_part, out_gain, final_weight):
    final_normed = layer_norm(inner_sum, out_gain).astype(jnp.bfloat16)
    product = jnp.dot(final_normed, final_weight.astype(jnp.bfloat16), preferred_element_type=jnp.float32)
    return (final_normed, product, product * gate_part)

def leave_back(inner_sum, gate_part, out_gain, final_weight, final_normed, product, grad_update):
    grad_product = (grad_update * gate_part).astype(jnp.bfloat16)
    grad_gate = grad_update * product
    grad_final = jnp.dot(final_normed.T, grad_product, preferred_element_type=jnp.float32)
    grad_normed = jnp.dot(grad_product, final_weight.astype(jnp.bfloat16).T, preferred_element_type=jnp.float32)
    unused, pull_norm = jax.vjp(layer_norm, inner_sum, out_gain)
    grad_inner, grad_gain = pull_norm(grad_normed)
    return (grad_inner, grad_gate, grad_gain, grad_final)

def one_complex(pair, cotangent, length, weights):
    outgo_norm, outgo_proj, outgo_gain, outgo_final, incom_norm, incom_proj, incom_gain, incom_final = weights
    tokens = pair.shape[0]
    channels = pair.shape[2]
    hidden = outgo_gain.shape[0]
    places = jnp.arange(tokens, dtype=jnp.int32)
    alive = (places < length).astype(jnp.float32)
    pair_mask = (alive[:, None] * alive[None, :]).reshape(-1, 1)
    flat_start = pair.reshape(-1, channels).astype(jnp.float32)
    normed_one, mixture_one, left_one, right_one, gate_one = entry(flat_start, outgo_norm, outgo_proj, pair_mask, hidden)
    left_first = rounded(left_one).reshape(tokens, tokens, hidden)
    right_first = rounded(right_one).reshape(tokens, tokens, hidden)
    inner_one = jnp.einsum('ikh,jkh->ijh', left_first, right_first).reshape(-1, hidden)
    final_one, product_one, update_one = leave(inner_one, gate_one, outgo_gain, outgo_final)
    flat_middle = rounded(flat_start + update_one)
    normed_two, mixture_two, left_two, right_two, gate_two = entry(flat_middle, incom_norm, incom_proj, pair_mask, hidden)
    left_second = rounded(left_two).reshape(tokens, tokens, hidden)
    right_second = rounded(right_two).reshape(tokens, tokens, hidden)
    inner_two = jnp.einsum('kih,kjh->ijh', left_second, right_second).reshape(-1, hidden)
    final_two, product_two, update_two = leave(inner_two, gate_two, incom_gain, incom_final)
    grad_end = cotangent.reshape(-1, channels).astype(jnp.float32)
    grad_inner_two, grad_gate_two, grad_gain_two, grad_final_two = leave_back(inner_two, gate_two, incom_gain, incom_final, final_two, product_two, grad_end)
    grad_cells_two = rounded(grad_inner_two).reshape(tokens, tokens, hidden)
    grad_left_two = jnp.einsum('ijh,kjh->kih', grad_cells_two, right_second).reshape(-1, hidden)
    grad_right_two = jnp.einsum('kih,ijh->kjh', left_second, grad_cells_two).reshape(-1, hidden)
    grad_flat_two, grad_norm_two, grad_proj_two = entry_back(flat_middle, incom_norm, incom_proj, pair_mask, hidden, normed_two, mixture_two, grad_left_two, grad_right_two, grad_gate_two)
    grad_middle = grad_end + grad_flat_two
    grad_inner_one, grad_gate_one, grad_gain_one, grad_final_one = leave_back(inner_one, gate_one, outgo_gain, outgo_final, final_one, product_one, grad_middle)
    grad_cells_one = rounded(grad_inner_one).reshape(tokens, tokens, hidden)
    grad_left_one = jnp.einsum('ijh,jkh->ikh', grad_cells_one, right_first).reshape(-1, hidden)
    grad_right_one = jnp.einsum('ijh,ikh->jkh', grad_cells_one, left_first).reshape(-1, hidden)
    grad_flat_one, grad_norm_one, grad_proj_one = entry_back(flat_start, outgo_norm, outgo_proj, pair_mask, hidden, normed_one, mixture_one, grad_left_one, grad_right_one, grad_gate_one)
    grad_begin = grad_middle + grad_flat_one
    grads = (grad_norm_one, grad_proj_one, grad_gain_one, grad_final_one, grad_norm_two, grad_proj_two, grad_gain_two, grad_final_two)
    return (grad_begin.reshape(tokens, tokens, channels), grads)

def reference(pair, cotangent, lengths, outgo_norm, outgo_proj, outgo_gain, outgo_final, incom_norm, incom_proj, incom_gain, incom_final):
    weights = (outgo_norm, outgo_proj, outgo_gain, outgo_final, incom_norm, incom_proj, incom_gain, incom_final)

    def advance(carry, items):
        grad_block, grads = one_complex(items[0], items[1], items[2], weights)
        return (jax.tree.map(lambda first, second: first + second, carry, grads), grad_block)
    zeros = tuple((jnp.zeros(weight.shape, jnp.float32) for weight in weights))
    totals, grad_pairs = lax.scan(advance, zeros, (pair, cotangent, lengths))
    scale = 1.0 / math.sqrt(N_DP * TOK * TOK)
    return (grad_pairs, totals[0] * scale, totals[1] * scale, totals[2] * scale, totals[3] * scale, totals[4] * scale, totals[5] * scale, totals[6] * scale, totals[7] * scale)
```

```python
import functools
import math

import jax
import jax.numpy as jnp
from jax import lax
from jax.experimental import pallas as pl
from jax.experimental.pallas import tpu as pltpu
from jax.sharding import PartitionSpec as P

EPSILON = 1e-05
MESH = pl.DeviceIdType.MESH
F32, BF16 = jnp.float32, jnp.bfloat16
PARTS = 32
DEPTH = 16
ROWS, TOK, C = 8, 256, 128
CHUNKS = 2
W = TOK // CHUNKS
BLOCKS = ROWS * CHUNKS
CELLS = ROWS * TOK
PIECE, LANES = 16, 384


def dot(a, b, ca=1, cb=0):
    return lax.dot_general(a, b, (((ca,), (cb,)), ((), ())), preferred_element_type=F32)


def sigmoid(v):
    return 0.5 * jnp.tanh(0.5 * v) + 0.5


def center(v):
    c = v - jnp.mean(v, axis=0, keepdims=True)
    rs = lax.rsqrt(jnp.mean(c * c, axis=0, keepdims=True) + EPSILON)
    return c * rs, rs


def center_back(grad, hat, rs):
    return rs * (
        grad
        - jnp.mean(grad, axis=0, keepdims=True)
        - hat * jnp.mean(grad * hat, axis=0, keepdims=True)
    )


def partner(me, s):
    u = s + s // 20
    dx, dy, dc = (2 + 3 * (u // 8)) % 4, (2 + 3 * ((u // 2) % 4)) % 4, u % 2
    x, y, c = me // 8, (me // 2) % 4, me % 2
    return ((x + dx) % 4) * 8 + ((y + dy) % 4) * 2 + (c + dc) % 2


def kernel(
    len_ref, pair_ref, cot_ref, n1_ref, p1_ref, g1_ref, f1_ref, n2_ref, p2_ref, g2_ref, f2_ref,
    out_ref, on1, op1, og1, of1, on2, op2, og2, of2,
    gnb, ggb, pjt, pj, fnt, fw, xt, ct, xh, rsx, st, nrm, gm, fnn, gp, ih, rsi, prod, acc_n, acc_g,
    tmp, sa, ra, sb, rb, tri, ws, wr, zs, zr, cs, cr, ssem, rsem,
):
    me = lax.axis_index("axial")
    depth_me = lax.axis_index("dp")
    length = len_ref[0]

    barrier = pltpu.get_barrier_semaphore()

    def hello(s, _):
        pl.semaphore_signal(barrier, inc=1, device_id={"axial": partner(me, s)}, device_id_type=MESH)
        return 0

    def hello_z(s, _):
        pl.semaphore_signal(
            barrier, inc=1, device_id={"dp": (depth_me + s) % DEPTH}, device_id_type=MESH
        )
        return 0

    lax.fori_loop(0, PARTS - 1, hello, 0)
    lax.fori_loop(1, DEPTH, hello_z, 0)

    for u, (n, p, g, f) in enumerate(
        ((n1_ref, p1_ref, g1_ref, f1_ref), (n2_ref, p2_ref, g2_ref, f2_ref))
    ):
        for vec, wide in ((n, gnb), (g, ggb)):
            col = jnp.broadcast_to(vec[...], (C, C)).T
            for k in range(W // C):
                wide[u, :, k * C : (k + 1) * C] = col
        pj[u] = p[...].astype(BF16)
        pjt[u] = p[...].T.astype(BF16)
        fw[u] = f[...].astype(BF16)
        fnt[u] = f[...].T.astype(BF16)
    acc_n[...] = jnp.zeros_like(acc_n)
    acc_g[...] = jnp.zeros_like(acc_g)

    def send(src, dst, k):
        dst[me] = src[me]

        def go(s, _):
            t = partner(me, s)
            pltpu.make_async_remote_copy(
                src_ref=src.at[t], dst_ref=dst.at[me], send_sem=ssem.at[k], recv_sem=rsem.at[k],
                device_id={"axial": t}, device_id_type=MESH,
            ).start()
            return 0

        lax.fori_loop(0, PARTS - 1, go, 0)

    def arrived(src, dst, k):
        part = pl.ds(0, PARTS - 1)
        pltpu.make_async_remote_copy(
            src_ref=src.at[part], dst_ref=dst.at[part], send_sem=ssem.at[k], recv_sem=rsem.at[k],
            device_id={"axial": partner(me, 0)}, device_id_type=MESH,
        ).wait()

    def rows(body):
        lax.fori_loop(0, ROWS, lambda r, _: (body(r), 0)[1], 0)

    def alive(q, r):
        col = lax.broadcasted_iota(jnp.int32, (1, W), 1) + q * W
        row = jnp.zeros((1, W), jnp.int32) + (me * ROWS + r)
        return jnp.where(jnp.maximum(col, row) < length, 1.0, 0.0)

    def cut(q, r):
        return pl.ds(pl.multiple_of((q * ROWS + r) * W, W), W)

    def strided(r):
        return pl.ds(r, C, stride=ROWS)

    def entry(u, q, r, x):
        b = q * ROWS + r
        hat, rs = center(x)
        xh[u, b] = hat
        rsx[u, b] = rs
        normed = (hat * gnb[u]).astype(BF16)
        nrm[u, :, cut(q, r)] = normed
        mask = alive(q, r)
        for side in range(2):
            value = dot(pjt[u, side * C : (side + 1) * C, :], normed)
            sig = sigmoid(dot(pjt[u, (2 + side) * C : (3 + side) * C, :], normed))
            st[u, b, side * C : (side + 1) * C, :] = value
            st[u, b, (2 + side) * C : (3 + side) * C, :] = sig
            tmp[side, strided(r), :] = value * sig * mask
        st[u, b, 4 * C :, :] = sigmoid(dot(pjt[u, 4 * C :, :], normed))

    def leave(u, q, r):
        b = q * ROWS + r
        hat, rs = center(tmp[0, strided(r), :])
        ih[u, b] = hat
        rsi[u, b] = rs
        normed = (hat * ggb[u]).astype(BF16)
        fnn[u, :, cut(q, r)] = normed
        product = dot(fnt[u], normed)
        prod[u, b] = product
        return product

    def leave_back(u, q, r, grad):
        b = q * ROWS + r
        gate = st[u, b, 4 * C :, :]
        grad_product = (grad * gate).astype(BF16)
        gp[u, :, cut(q, r)] = grad_product
        gm[u, 4 * C :, cut(q, r)] = (grad * prod[u, b] * gate * (1.0 - gate)).astype(BF16)
        grad_normed = dot(fw[u], grad_product)
        hat = ih[u, b]
        acc_g[u] += grad_normed * hat
        tmp[0, strided(r), :] = center_back(grad_normed * ggb[u], hat, rsi[u, b])

    def entry_back(u, q, r):
        b = q * ROWS + r
        mask = alive(q, r)
        for side in range(2):
            grad = tmp[side, strided(r), :] * mask
            value = st[u, b, side * C : (side + 1) * C, :]
            sig = st[u, b, (2 + side) * C : (3 + side) * C, :]
            through = grad * sig
            gm[u, side * C : (side + 1) * C, cut(q, r)] = through.astype(BF16)
            gm[u, (2 + side) * C : (3 + side) * C, cut(q, r)] = (
                through * value * (1.0 - sig)
            ).astype(BF16)
        grad_normed = dot(pj[u], gm[u, :, cut(q, r)])
        hat = xh[u, b]
        acc_n[u] += grad_normed * hat
        return center_back(grad_normed * gnb[u], hat, rsx[u, b])

    def pack(dst, sides):
        def one(d, _):
            for side in range(sides):
                dst[d, side * 32 : (side + 1) * 32, :] = tmp[
                    side, pl.ds(pl.multiple_of(d * 32, 32), 32), :
                ].astype(BF16)
            return 0

        lax.fori_loop(0, PARTS, one, 0)

    def unpack(src, sides):
        def one(d, _):
            for side in range(sides):
                tmp[side, pl.ds(pl.multiple_of(d * 32, 32), 32), :] = src[
                    d, side * 32 : (side + 1) * 32, :
                ].astype(F32)
            return 0

        lax.fori_loop(0, PARTS, one, 0)

    def channels(ref, base, h):
        parts = [
            ref[q, :, base + 16 * h : base + 16 * h + 16, :].astype(F32).reshape(PARTS, 2, ROWS, W)
            for q in range(CHUNKS)
        ]
        return [
            jnp.concatenate([p[:, e].reshape(TOK, W) for p in parts], axis=1).astype(BF16)
            for e in range(2)
        ]

    def put(dst, base, h, both):
        both = jnp.concatenate([m.reshape(PARTS, ROWS, TOK) for m in both], axis=1).astype(BF16)
        for q in range(CHUNKS):
            dst[q, :, base + 16 * h : base + 16 * h + 16, :] = both[:, :, q * W : (q + 1) * W]

    def phase(k, q):
        return k * CHUNKS + q

    pl.semaphore_wait(barrier, PARTS - 1 + DEPTH - 1)
    for q in range(CHUNKS):

        def first(r):
            x = pair_ref[r, q * W : (q + 1) * W, :].astype(F32).T
            xt[q * ROWS + r] = x
            entry(0, q, r, x)

        rows(first)
        pack(sa.at[0, q], 2)
        send(sa.at[0, q], ra.at[0, q], phase(0, q))

    for q in range(CHUNKS):

        def turn(r):
            ct[q * ROWS + r] = cot_ref[r, q * W : (q + 1) * W, :].astype(F32).T

        rows(turn)

    def forward_triangle(u, src, dst, k):
        for q in range(CHUNKS):
            arrived(sa.at[src, q], ra.at[src, q], phase(k - 1, q))
        for h in range(2):
            left, right = channels(ra.at[src], 0, h), channels(ra.at[src], 32, h)
            for e in range(2):
                tri[u, 0, 2 * h + e] = left[e]
                tri[u, 1, 2 * h + e] = right[e]
            contract = 1 - u
            put(sb.at[dst], 0, h, [dot(left[e], right[e], contract, contract) for e in range(2)])
        for q in range(CHUNKS):
            send(sb.at[dst, q], rb.at[dst, q], phase(k, q))

    def backward_triangle(u, src, dst, k):
        for q in range(CHUNKS):
            arrived(sb.at[src, q], rb.at[src, q], phase(k - 1, q))
        for h in range(2):
            grad = channels(rb.at[src], 0, h)
            left = [tri[u, 0, 2 * h + e] for e in range(2)]
            right = [tri[u, 1, 2 * h + e] for e in range(2)]
            if u == 0:
                grad_left = [dot(grad[e], right[e]) for e in range(2)]
                grad_right = [dot(grad[e], left[e], 0, 0) for e in range(2)]
            else:
                grad_left = [dot(right[e], grad[e], 1, 1) for e in range(2)]
                grad_right = [dot(left[e], grad[e]) for e in range(2)]
            put(sa.at[dst], 0, h, grad_left)
            put(sa.at[dst], 32, h, grad_right)
        for q in range(CHUNKS):
            send(sa.at[dst, q], ra.at[dst, q], phase(k, q))

    forward_triangle(0, 0, 0, 1)

    for q in range(CHUNKS):
        arrived(sb.at[0, q], rb.at[0, q], phase(1, q))
        unpack(rb.at[0, q], 1)

        def second(r):
            b = q * ROWS + r
            product = leave(0, q, r)
            middle = (xt[b] + product * st[0, b, 4 * C :, :]).astype(BF16).astype(F32)
            entry(1, q, r, middle)

        rows(second)
        pack(sa.at[1, q], 2)
        send(sa.at[1, q], ra.at[1, q], phase(2, q))

    forward_triangle(1, 1, 1, 3)

    for q in range(CHUNKS):
        arrived(sb.at[1, q], rb.at[1, q], phase(3, q))
        unpack(rb.at[1, q], 1)

        def third(r):
            leave(1, q, r)
            leave_back(1, q, r, ct[q * ROWS + r])

        rows(third)
        pack(sb.at[2, q], 1)
        send(sb.at[2, q], rb.at[2, q], phase(4, q))

    backward_triangle(1, 2, 2, 5)

    for q in range(CHUNKS):
        arrived(sa.at[2, q], ra.at[2, q], phase(5, q))
        unpack(ra.at[2, q], 2)

        def fourth(r):
            b = q * ROWS + r
            grad = ct[b] + entry_back(1, q, r)
            ct[b] = grad
            leave_back(0, q, r, grad)

        rows(fourth)
        pack(sb.at[3, q], 1)
        send(sb.at[3, q], rb.at[3, q], phase(6, q))

    def weight_grads(u):
        proj = dot(nrm[u], gm[u], 1, 1)
        final = dot(fnn[u], gp[u], 1, 1)
        low, high = proj[:, :LANES], jnp.concatenate([proj[:, LANES:], final], axis=1)
        for i in range(C // PIECE):
            ws[i * 4 + 2 * u, :, :LANES] = low[i * PIECE : (i + 1) * PIECE].astype(BF16)
            ws[i * 4 + 2 * u + 1, :, :LANES] = high[i * PIECE : (i + 1) * PIECE].astype(BF16)

    def gain_row(acc):
        total = acc[:, :C]
        for k in range(1, W // C):
            total = total + acc[:, k * C : (k + 1) * C]
        return jnp.sum(total.T, axis=0, keepdims=True)

    weight_grads(1)

    backward_triangle(0, 3, 3, 7)

    for q in range(CHUNKS):
        arrived(sa.at[3, q], ra.at[3, q], phase(7, q))
        unpack(ra.at[3, q], 2)

        def fifth(r):
            grad = ct[q * ROWS + r] + entry_back(0, q, r)
            out_ref[r, q * W : (q + 1) * W, :] = grad.T

        rows(fifth)

    weight_grads(0)
    gains = [gain_row(acc_n[0]), gain_row(acc_g[0]), gain_row(acc_n[1]), gain_row(acc_g[1])]
    gains = jnp.concatenate(gains + [jnp.zeros((PIECE - 4, C), F32)], axis=0).astype(BF16)

    def spread(d, _):
        ws[d, :, LANES:] = gains
        return 0

    lax.fori_loop(0, PARTS, spread, 0)
    last = 8 * CHUNKS
    send(ws, wr, last)
    arrived(ws, wr, last)

    def add(ref):
        return lambda d, total: total + ref[d].astype(F32)

    zs[...] = lax.fori_loop(0, PARTS, add(wr), jnp.zeros((PIECE, LANES + C), F32)).astype(BF16)
    zr[depth_me] = zs[...]

    def go_z(s, _):
        pltpu.make_async_remote_copy(
            src_ref=zs, dst_ref=zr.at[depth_me], send_sem=ssem.at[last + 1],
            recv_sem=rsem.at[last + 1],
            device_id={"dp": (depth_me + s) % DEPTH}, device_id_type=MESH,
        ).start()
        return 0

    lax.fori_loop(1, DEPTH, go_z, 0)
    part = pl.ds(0, DEPTH - 1)
    pltpu.make_async_remote_copy(
        src_ref=zr.at[part], dst_ref=zr.at[part], send_sem=ssem.at[last + 1],
        recv_sem=rsem.at[last + 1],
        device_id={"dp": (depth_me + 1) % DEPTH}, device_id_type=MESH,
    ).wait()
    scale = 1.0 / math.sqrt(DEPTH * TOK * TOK)
    total = lax.fori_loop(0, DEPTH, add(zr), jnp.zeros((PIECE, LANES + C), F32)) * scale
    for k, ref in enumerate((on1, og1, on2, og2)):
        ref[...] = total[k : k + 1, LANES:]
    cs[...] = total[:, :LANES].astype(BF16)
    cr[me] = cs[...]

    def go_c(s, _):
        pltpu.make_async_remote_copy(
            src_ref=cs, dst_ref=cr.at[me], send_sem=ssem.at[last + 2], recv_sem=rsem.at[last + 2],
            device_id={"axial": partner(me, s)}, device_id_type=MESH,
        ).start()
        return 0

    lax.fori_loop(0, PARTS - 1, go_c, 0)
    arrived(cr, cr, last + 2)
    for u, (proj, final) in enumerate(((op1, of1), (op2, of2))):
        for i in range(C // PIECE):
            here = slice(i * PIECE, (i + 1) * PIECE)
            proj[here, :LANES] = cr[i * 4 + 2 * u].astype(F32)
            high = cr[i * 4 + 2 * u + 1].astype(F32)
            proj[here, LANES:] = high[:, : 5 * C - LANES]
            final[here, :] = high[:, 5 * C - LANES :]


def body(pair, cotangent, lengths, *weights):
    weights = [w.reshape(1, C) if w.ndim == 1 else w for w in weights]
    vmem = pl.BlockSpec(memory_space=pltpu.VMEM)
    sums = [jax.ShapeDtypeStruct(w.shape, F32) for w in weights]
    outs = pl.pallas_call(
        kernel,
        out_shape=[jax.ShapeDtypeStruct((ROWS, TOK, C), F32)] + sums,
        in_specs=[pl.BlockSpec(memory_space=pltpu.SMEM)] + [vmem] * 10,
        out_specs=[vmem] * 9,
        scratch_shapes=[
            pltpu.VMEM((2, C, W), F32),
            pltpu.VMEM((2, C, W), F32),
            pltpu.VMEM((2, 5 * C, C), BF16),
            pltpu.VMEM((2, C, 5 * C), BF16),
            pltpu.VMEM((2, C, C), BF16),
            pltpu.VMEM((2, C, C), BF16),
            pltpu.VMEM((BLOCKS, C, W), F32),
            pltpu.VMEM((BLOCKS, C, W), F32),
            pltpu.VMEM((2, BLOCKS, C, W), F32),
            pltpu.VMEM((2, BLOCKS, 1, W), F32),
            pltpu.VMEM((2, BLOCKS, 5 * C, W), F32),
            pltpu.VMEM((2, C, CELLS), BF16),
            pltpu.VMEM((2, 5 * C, CELLS), BF16),
            pltpu.VMEM((2, C, CELLS), BF16),
            pltpu.VMEM((2, C, CELLS), BF16),
            pltpu.VMEM((2, BLOCKS, C, W), F32),
            pltpu.VMEM((2, BLOCKS, 1, W), F32),
            pltpu.VMEM((2, BLOCKS, C, W), F32),
            pltpu.VMEM((2, C, W), F32),
            pltpu.VMEM((2, C, W), F32),
            pltpu.VMEM((2, C * ROWS, W), F32),
            pltpu.VMEM((4, CHUNKS, PARTS, 64, W), BF16),
            pltpu.VMEM((4, CHUNKS, PARTS, 64, W), BF16),
            pltpu.VMEM((4, CHUNKS, PARTS, 32, W), BF16),
            pltpu.VMEM((4, CHUNKS, PARTS, 32, W), BF16),
            pltpu.VMEM((2, 2, 4, TOK, TOK), BF16),
            pltpu.VMEM((PARTS, PIECE, LANES + C), BF16),
            pltpu.VMEM((PARTS, PIECE, LANES + C), BF16),
            pltpu.VMEM((PIECE, LANES + C), BF16),
            pltpu.VMEM((DEPTH, PIECE, LANES + C), BF16),
            pltpu.VMEM((PIECE, LANES), BF16),
            pltpu.VMEM((PARTS, PIECE, LANES), BF16),
            pltpu.SemaphoreType.DMA((8 * CHUNKS + 3,)),
            pltpu.SemaphoreType.DMA((8 * CHUNKS + 3,)),
        ],
        compiler_params=pltpu.CompilerParams(
            collective_id=0, has_side_effects=True, vmem_limit_bytes=60 << 20
        ),
    )(lengths, pair[0], cotangent[0], *weights)
    grads = [o.reshape(C) if o.shape[0] == 1 else o for o in outs[1:]]
    return (outs[0][None], *grads)


def solution(mesh):
    return jax.shard_map(
        body,
        mesh=mesh,
        in_specs=(P("dp", "axial", None, None), P("dp", "axial", None, None), P("dp")) + (P(),) * 8,
        out_specs=(P("dp", "axial", None, None),) + (P(),) * 8,
        check_vma=False,
    )
```

```python
import functools
import math

import jax
import jax.numpy as jnp
from jax import lax
from jax.experimental import pallas as pl
from jax.experimental.pallas import tpu as pltpu
from jax.sharding import PartitionSpec as P

EPSILON = 1e-05
MESH = pl.DeviceIdType.MESH
F32, BF16 = jnp.float32, jnp.bfloat16
PARTS = 32
DEPTH = 16
ROWS, TOK, C = 8, 256, 128
CHUNKS = 2
W = TOK // CHUNKS
BLOCKS = ROWS * CHUNKS
CELLS = ROWS * TOK
PIECE = 16
EARLY, LATE = 256, 128


def dot(a, b, ca=1, cb=0):
    return lax.dot_general(a, b, (((ca,), (cb,)), ((), ())), preferred_element_type=F32)


def sigmoid(v):
    return 0.5 * jnp.tanh(0.5 * v) + 0.5


def center(v):
    c = v - jnp.mean(v, axis=0, keepdims=True)
    rs = lax.rsqrt(jnp.mean(c * c, axis=0, keepdims=True) + EPSILON)
    return c * rs, rs


def center_back(grad, hat, rs):
    return rs * (
        grad
        - jnp.mean(grad, axis=0, keepdims=True)
        - hat * jnp.mean(grad * hat, axis=0, keepdims=True)
    )


def partner(me, s):
    u = s + lax.div(s, 20)
    ox, oy, oc = lax.div(u, 8), lax.rem(lax.div(u, 2), 4), lax.rem(u, 2)
    x, y, c = lax.div(me, 8), lax.rem(lax.div(me, 2), 4), lax.rem(me, 2)
    x, y, c = lax.rem(x + 2 + 3 * ox, 4), lax.rem(y + 2 + 3 * oy, 4), lax.rem(c + oc, 2)
    return x * 8 + y * 2 + c


def kernel(
    len_ref, pair_hbm, cot_hbm, n1_hbm, p1_hbm, g1_hbm, f1_hbm, n2_hbm, p2_hbm, g2_hbm, f2_hbm,
    out_hbm, early_out, late_out,
    pair_ref, cot_ref, n_in, p_in, g_in, f_in, out_ref,
    gnb, ggb, pjt, pj, fnt, fw, xt, ct, xh, rsx, st, nrm, gm, fnn, gp, ih, rsi, prod,
    tmp, s2, r2, s1, r1, t1, u1, t2, u2, tri, es, er, ezs, ezr, ecs, ecr, ls, lr, lzs, lzr, lcs, lcr,
    ssem, rsem, isem, osem,
):
    me = lax.axis_index("axial")
    depth_me = lax.axis_index("dp")
    length = len_ref[0]

    barrier = pltpu.get_barrier_semaphore()

    def hello(s, _):
        pl.semaphore_signal(barrier, inc=1, device_id={"axial": partner(me, s)}, device_id_type=MESH)
        return 0

    def hello_z(s, _):
        pl.semaphore_signal(
            barrier, inc=1, device_id={"dp": (depth_me + s) % DEPTH}, device_id_type=MESH
        )
        return 0

    lax.fori_loop(0, PARTS - 1, hello, 0)
    lax.fori_loop(1, DEPTH, hello_z, 0)

    loads = [(pair_hbm, pair_ref), (cot_hbm, cot_ref)]
    for u, group in enumerate(
        ((n1_hbm, p1_hbm, g1_hbm, f1_hbm), (n2_hbm, p2_hbm, g2_hbm, f2_hbm))
    ):
        loads += [(h, v.at[u]) for h, v in zip(group, (n_in, p_in, g_in, f_in))]
    loads = [pltpu.make_async_copy(h, v, isem.at[i]) for i, (h, v) in enumerate(loads)]
    for i in (2, 3, 0, 4, 5, 6, 7, 8, 9, 1):
        loads[i].start()

    def weights(u):
        for k in range(4):
            loads[2 + 4 * u + k].wait()
        for vec, wide in ((n_in, gnb), (g_in, ggb)):
            wide[u] = jnp.broadcast_to(vec[u], (C, C)).T
        pj[u] = p_in[u].astype(BF16)
        pjt[u] = p_in[u].T.astype(BF16)
        fw[u] = f_in[u].astype(BF16)
        fnt[u] = f_in[u].T.astype(BF16)

    weights(0)
    loads[0].wait()

    def send(src, dst, k):
        dst[me] = src[me]

        def go(s, _):
            t = partner(me, s)
            pltpu.make_async_remote_copy(
                src_ref=src.at[t], dst_ref=dst.at[me], send_sem=ssem.at[k], recv_sem=rsem.at[k],
                device_id={"axial": t}, device_id_type=MESH,
            ).start()
            return 0

        lax.fori_loop(0, PARTS - 1, go, 0)

    def arrived(src, dst, k):
        part = pl.ds(0, PARTS - 1)
        pltpu.make_async_remote_copy(
            src_ref=src.at[part], dst_ref=dst.at[part], send_sem=ssem.at[k], recv_sem=rsem.at[k],
            device_id={"axial": partner(me, 0)}, device_id_type=MESH,
        ).wait()

    def rows(body):
        lax.fori_loop(0, ROWS, lambda r, _: (body(r), 0)[1], 0, unroll=4)

    def alive(q, r):
        col = lax.broadcasted_iota(jnp.int32, (1, W), 1) + q * W
        row = jnp.zeros((1, W), jnp.int32) + (me * ROWS + r)
        return jnp.where(jnp.maximum(col, row) < length, 1.0, 0.0)

    def cut(q, r):
        return pl.ds(pl.multiple_of((q * ROWS + r) * W, W), W)

    def strided(r):
        return pl.ds(r, C, stride=ROWS)

    def entry(u, q, r, x):
        b = q * ROWS + r
        hat, rs = center(x)
        xh[u, b] = hat
        rsx[u, b] = rs
        normed = (hat * gnb[u]).astype(BF16)
        nrm[u, :, cut(q, r)] = normed
        mask = alive(q, r)
        for side in range(2):
            value = dot(pjt[u, side * C : (side + 1) * C, :], normed)
            sig = sigmoid(dot(pjt[u, (2 + side) * C : (3 + side) * C, :], normed))
            st[u, b, side * C : (side + 1) * C, :] = value
            st[u, b, (2 + side) * C : (3 + side) * C, :] = sig
            tmp[side, strided(r), :] = value * sig * mask
        st[u, b, 4 * C :, :] = sigmoid(dot(pjt[u, 4 * C :, :], normed))

    def leave(u, q, r):
        b = q * ROWS + r
        hat, rs = center(tmp[0, strided(r), :])
        ih[u, b] = hat
        rsi[u, b] = rs
        normed = (hat * ggb[u]).astype(BF16)
        fnn[u, :, cut(q, r)] = normed
        product = dot(fnt[u], normed)
        prod[u, b] = product
        return product

    def leave_back(u, q, r, grad):
        b = q * ROWS + r
        gate = st[u, b, 4 * C :, :]
        grad_product = (grad * gate).astype(BF16)
        gp[u, :, cut(q, r)] = grad_product
        gm[u, 4 * C :, cut(q, r)] = (grad * prod[u, b] * gate * (1.0 - gate)).astype(BF16)
        grad_normed = dot(fw[u], grad_product)
        hat = ih[u, b]
        tmp[0, strided(r), :] = center_back(grad_normed * ggb[u], hat, rsi[u, b])

    def gating_back(u, q, r):
        b = q * ROWS + r
        mask = alive(q, r)
        for side in range(2):
            grad = tmp[side, strided(r), :] * mask
            value = st[u, b, side * C : (side + 1) * C, :]
            sig = st[u, b, (2 + side) * C : (3 + side) * C, :]
            through = grad * sig
            gm[u, side * C : (side + 1) * C, cut(q, r)] = through.astype(BF16)
            gm[u, (2 + side) * C : (3 + side) * C, cut(q, r)] = (
                through * value * (1.0 - sig)
            ).astype(BF16)

    def entry_back(u, q, r):
        b = q * ROWS + r
        grad_normed = dot(pj[u], gm[u, :, cut(q, r)])
        hat = xh[u, b]
        return center_back(grad_normed * gnb[u], hat, rsx[u, b])

    def pack(dst, q, sides):
        def one(d, _):
            for p in range(2):
                for side in range(sides):
                    dst[q, d, p, side * 16 : (side + 1) * 16, :] = tmp[
                        side, pl.ds(pl.multiple_of(d * 32 + p * 16, 16), 16), :
                    ].astype(BF16)
            return 0

        lax.fori_loop(0, PARTS, one, 0, unroll=4)

    def unpack(src, q, sides):
        def one(d, _):
            for p in range(2):
                for side in range(sides):
                    tmp[side, pl.ds(pl.multiple_of(d * 32 + p * 16, 16), 16), :] = src[
                        p, d, q, side * 16 : (side + 1) * 16, :
                    ].astype(F32)
            return 0

        lax.fori_loop(0, PARTS, one, 0, unroll=4)

    def send_part(src, dst, k, part):
        if part == 0:
            send(src.at[0], dst.at[0], 3 * k)
        else:
            send(src.at[1, :, part - 1], dst.at[1, :, part - 1], 3 * k + part)

    def arrived_part(src, dst, k, part):
        if part == 0:
            arrived(src.at[0], dst.at[0], 3 * k)
        else:
            arrived(src.at[1, :, part - 1], dst.at[1, :, part - 1], 3 * k + part)

    def send_chunk(src, dst, k, chunk):
        for part in ((0,), (1, 2))[chunk]:
            send_part(src, dst, k, part)

    def arrived_half(src, dst, k, half):
        for part in ((0, 1), (2,))[half]:
            arrived_part(src, dst, k, part)

    def channels(ref, side, p, q, to):
        block = ref[q, :, p, 16 * side : 16 * side + 16, :].astype(F32)
        block = block.reshape(PARTS, 2, ROWS, W)
        for e in range(2):
            to[2 * p + e, :, q * W : (q + 1) * W] = block[:, e].reshape(TOK, W).astype(BF16)

    def put(dst, side, p, both):
        both = jnp.concatenate([m.reshape(PARTS, ROWS, TOK) for m in both], axis=1).astype(BF16)
        for q in range(CHUNKS):
            dst[p, :, q, 16 * side : 16 * side + 16, :] = both[:, :, q * W : (q + 1) * W]

    for q in range(CHUNKS):

        def first(r):
            x = pair_ref[r, q * W : (q + 1) * W, :].astype(F32).T
            xt[q * ROWS + r] = x
            entry(0, q, r, x)

        rows(first)
        pack(s2.at[0], q, 2)
        if q == 0:
            pl.semaphore_wait(barrier, PARTS - 1 + DEPTH - 1)
        send_chunk(s2.at[0], r2.at[0], 0, q)

    weights(1)
    loads[1].wait()

    for q in range(CHUNKS):

        def turn(r):
            ct[q * ROWS + r] = cot_ref[r, q * W : (q + 1) * W, :].astype(F32).T

        rows(turn)

    def forward_triangle(u, k):
        src, dst = (s2.at[u], r2.at[u]), (t1.at[u], u1.at[u])
        arrived_part(*src, k - 1, 0)
        for p in range(2):
            for side in range(2):
                channels(src[1], side, p, 0, tri.at[u, side])
        for p in range(2):
            arrived_part(*src, k - 1, 1 + p)
            for side in range(2):
                channels(src[1], side, p, 1, tri.at[u, side])
            both = [
                dot(tri[u, 0, 2 * p + e], tri[u, 1, 2 * p + e], 1 - u, 1 - u) for e in range(2)
            ]
            put(dst[0], 0, p, both)
            send_chunk(*dst, k, p)

    def backward_triangle(u, k):
        src, dst = (s1.at[u], r1.at[u]), (t2.at[u], u2.at[u])
        arrived_part(*src, k - 1, 0)
        for p in range(2):
            channels(src[1], 0, p, 0, tri.at[2, 0])
        for p in range(2):
            arrived_part(*src, k - 1, 1 + p)
            channels(src[1], 0, p, 1, tri.at[2, 0])
            grad = [tri[2, 0, 2 * p + e] for e in range(2)]
            left = [tri[u, 0, 2 * p + e] for e in range(2)]
            right = [tri[u, 1, 2 * p + e] for e in range(2)]
            if u == 0:
                grad_left = [dot(grad[e], right[e]) for e in range(2)]
                grad_right = [dot(grad[e], left[e], 0, 0) for e in range(2)]
            else:
                grad_left = [dot(right[e], grad[e], 1, 1) for e in range(2)]
                grad_right = [dot(left[e], grad[e]) for e in range(2)]
            put(dst[0], 0, p, grad_left)
            put(dst[0], 1, p, grad_right)
            send_chunk(*dst, k, p)

    forward_triangle(0, 1)

    for q in range(CHUNKS):
        arrived_half(t1.at[0], u1.at[0], 1, q)
        unpack(u1.at[0], q, 1)

        def second(r):
            b = q * ROWS + r
            product = leave(0, q, r)
            middle = (xt[b] + product * st[0, b, 4 * C :, :]).astype(BF16).astype(F32)
            entry(1, q, r, middle)

        rows(second)
        pack(s2.at[1], q, 2)
        send_chunk(s2.at[1], r2.at[1], 2, q)

    forward_triangle(1, 3)

    for q in range(CHUNKS):
        arrived_half(t1.at[1], u1.at[1], 3, q)
        unpack(u1.at[1], q, 1)

        def third(r):
            leave(1, q, r)
            leave_back(1, q, r, ct[q * ROWS + r])

        rows(third)
        pack(s1.at[1], q, 1)
        send_chunk(s1.at[1], r1.at[1], 4, q)

    backward_triangle(1, 5)

    for q in range(CHUNKS):
        arrived_half(t2.at[1], u2.at[1], 5, q)
        unpack(u2.at[1], q, 2)

        def fourth(r):
            b = q * ROWS + r
            gating_back(1, q, r)
            grad = ct[b] + entry_back(1, q, r)
            ct[b] = grad
            leave_back(0, q, r, grad)

        rows(fourth)
        pack(s1.at[0], q, 1)
        send_chunk(s1.at[0], r1.at[0], 6, q)

    last = 8 * 3

    def pieces(to, grads):
        wide = grads.shape[1] // 4
        for d in range(PARTS):
            here = grads[d // 4 * PIECE : (d // 4 + 1) * PIECE, d % 4 * wide : (d % 4 + 1) * wide]
            to[d] = here.astype(BF16)

    def total(ref):
        rest = range(1, ref.shape[0])
        return functools.reduce(lambda a, d: a + ref[d].astype(F32), rest, ref[0].astype(F32))

    def send_z(src, dst, k):
        dst[depth_me] = src[...]

        def go(s, _):
            pltpu.make_async_remote_copy(
                src_ref=src, dst_ref=dst.at[depth_me], send_sem=ssem.at[k], recv_sem=rsem.at[k],
                device_id={"dp": lax.rem(depth_me + s, DEPTH)}, device_id_type=MESH,
            ).start()
            return 0

        lax.fori_loop(1, DEPTH, go, 0)

    def arrived_z(dst, k):
        part = pl.ds(0, DEPTH - 1)
        pltpu.make_async_remote_copy(
            src_ref=dst.at[part], dst_ref=dst.at[part], send_sem=ssem.at[k], recv_sem=rsem.at[k],
            device_id={"dp": lax.rem(depth_me + 1, DEPTH)}, device_id_type=MESH,
        ).wait()

    def send_all(src, dst, k):
        dst[me] = src[...]

        def go(s, _):
            pltpu.make_async_remote_copy(
                src_ref=src, dst_ref=dst.at[me], send_sem=ssem.at[k], recv_sem=rsem.at[k],
                device_id={"axial": partner(me, s)}, device_id_type=MESH,
            ).start()
            return 0

        lax.fori_loop(0, PARTS - 1, go, 0)

    early = [
        dot(nrm[1], gm[1], 1, 1),
        dot(fnn[1], gp[1], 1, 1),
        dot(nrm[0], gm[0, 4 * C :, :], 1, 1),
        dot(fnn[0], gp[0], 1, 1),
    ]
    pieces(es, jnp.concatenate(early, axis=1))
    send(es, er, last)

    backward_triangle(0, 7)

    arrived(es, er, last)
    ezs[...] = total(er).astype(BF16)
    send_z(ezs, ezr, last + 1)

    def store(q):
        here = (slice(None), pl.ds(q * W, W))
        return pltpu.make_async_copy(out_ref.at[here], out_hbm.at[here], osem.at[q])

    def fifth(q, r):
        grad = ct[q * ROWS + r] + entry_back(0, q, r)
        out_ref[r, q * W : (q + 1) * W, :] = grad.T

    for q in range(CHUNKS):
        arrived_half(t2.at[0], u2.at[0], 7, q)
        unpack(u2.at[0], q, 2)
        rows(functools.partial(gating_back, 0, q))
        if q == 0:
            rows(functools.partial(fifth, q))
            store(q).start()

    scale = 1.0 / math.sqrt(DEPTH * TOK * TOK)
    pieces(ls, dot(nrm[0], gm[0, : 4 * C, :], 1, 1))
    send(ls, lr, last + 3)
    rows(functools.partial(fifth, 1))
    store(1).start()
    arrived_z(ezr, last + 1)
    ecs[...] = (total(ezr) * scale).astype(BF16)
    arrived(ls, lr, last + 3)
    lzs[...] = total(lr).astype(BF16)
    send_z(lzs, lzr, last + 4)
    send_all(ecs, ecr, last + 2)
    arrived_z(lzr, last + 4)
    lcs[...] = (total(lzr) * scale).astype(BF16)
    send_all(lcs, lcr, last + 5)
    arrived(ecr, ecr, last + 2)
    early_out[...] = ecr[...]
    for q in range(CHUNKS):
        store(q).wait()
    arrived(lcr, lcr, last + 5)
    late_out[...] = lcr[...]


def finish(
    big, early, late, n1, p1, g1, f1, n2, p2, g2, f2, out, on1, op1, og1, of1, on2, op2, og2, of2
):
    out[...] = big[...]
    for i in range(C // PIECE):
        here = slice(i * PIECE, (i + 1) * PIECE)
        blocks = [early[4 * i + j].astype(F32) for j in range(4)]
        for j in range(4):
            op1[here, j * LATE : (j + 1) * LATE] = late[4 * i + j].astype(F32)
        op1[here, 4 * C :] = blocks[3][:, :C]
        of1[here, :] = blocks[3][:, C:]
        op2[here, : 2 * C] = blocks[0]
        op2[here, 2 * C : 4 * C] = blocks[1]
        op2[here, 4 * C :] = blocks[2][:, :C]
        of2[here, :] = blocks[2][:, C:]

    def gain(to, by, weight, grad):
        both = weight[...].astype(BF16).astype(F32) * grad[...]
        both = sum(both[:, j * C : (j + 1) * C] for j in range(both.shape[1] // C))
        to[...] = jnp.sum(both.T, axis=0, keepdims=True) / by[...]

    gain(on1, n1, p1, op1)
    gain(og1, g1, f1, of1)
    gain(on2, n2, p2, op2)
    gain(og2, g2, f2, of2)


def body(pair, cotangent, lengths, *weights):
    weights = [w.reshape(1, C) if w.ndim == 1 else w for w in weights]
    vmem = pl.BlockSpec(memory_space=pltpu.VMEM)
    sums = [jax.ShapeDtypeStruct(w.shape, F32) for w in weights]
    hbm = pl.BlockSpec(memory_space=pl.ANY)
    parts = pl.pallas_call(
        kernel,
        out_shape=[
            jax.ShapeDtypeStruct((ROWS, TOK, C), F32),
            jax.ShapeDtypeStruct((PARTS, PIECE, EARLY), BF16),
            jax.ShapeDtypeStruct((PARTS, PIECE, LATE), BF16),
        ],
        in_specs=[pl.BlockSpec(memory_space=pltpu.SMEM)] + [hbm] * 10,
        out_specs=[hbm, vmem, vmem],
        scratch_shapes=[
            pltpu.VMEM((ROWS, TOK, C), BF16),
            pltpu.VMEM((ROWS, TOK, C), BF16),
            pltpu.VMEM((2, 1, C), F32),
            pltpu.VMEM((2, C, 5 * C), F32),
            pltpu.VMEM((2, 1, C), F32),
            pltpu.VMEM((2, C, C), F32),
            pltpu.VMEM((ROWS, TOK, C), F32),
            pltpu.VMEM((2, C, W), F32),
            pltpu.VMEM((2, C, W), F32),
            pltpu.VMEM((2, 5 * C, C), BF16),
            pltpu.VMEM((2, C, 5 * C), BF16),
            pltpu.VMEM((2, C, C), BF16),
            pltpu.VMEM((2, C, C), BF16),
            pltpu.VMEM((BLOCKS, C, W), F32),
            pltpu.VMEM((BLOCKS, C, W), F32),
            pltpu.VMEM((2, BLOCKS, C, W), F32),
            pltpu.VMEM((2, BLOCKS, 1, W), F32),
            pltpu.VMEM((2, BLOCKS, 5 * C, W), F32),
            pltpu.VMEM((2, C, CELLS), BF16),
            pltpu.VMEM((2, 5 * C, CELLS), BF16),
            pltpu.VMEM((2, C, CELLS), BF16),
            pltpu.VMEM((2, C, CELLS), BF16),
            pltpu.VMEM((2, BLOCKS, C, W), F32),
            pltpu.VMEM((2, BLOCKS, 1, W), F32),
            pltpu.VMEM((2, BLOCKS, C, W), F32),
            pltpu.VMEM((2, C * ROWS, W), F32),
        ]
        + [
            pltpu.VMEM((2, 2, PARTS, 2, 16 * sides, W), BF16)
            for sides in (2, 2, 1, 1, 1, 1, 2, 2)
        ]
        + [
            pltpu.VMEM((3, 2, 4, TOK, TOK), BF16),
        ]
        + [
            pltpu.VMEM(shape + (PIECE, wide), BF16)
            for wide in (EARLY, LATE)
            for shape in ((PARTS,), (PARTS,), (), (DEPTH,), (), (PARTS,))
        ]
        + [
            pltpu.SemaphoreType.DMA((8 * 3 + 6,)),
            pltpu.SemaphoreType.DMA((8 * 3 + 6,)),
            pltpu.SemaphoreType.DMA((10,)),
            pltpu.SemaphoreType.DMA((CHUNKS,)),
        ],
        compiler_params=pltpu.CompilerParams(
            collective_id=0, has_side_effects=True, vmem_limit_bytes=60 << 20
        ),
    )(lengths, pair[0], cotangent[0], *weights)
    outs = pl.pallas_call(
        finish,
        out_shape=[jax.ShapeDtypeStruct((ROWS, TOK, C), F32)] + sums,
        in_specs=[vmem] * 11,
        out_specs=[vmem] * 9,
        compiler_params=pltpu.CompilerParams(vmem_limit_bytes=60 << 20),
    )(*parts, *weights)
    grads = [o.reshape(C) if o.shape[0] == 1 else o for o in outs[1:]]
    return (outs[0][None], *grads)


def solution(mesh):
    return jax.shard_map(
        body,
        mesh=mesh,
        in_specs=(P("dp", "axial", None, None), P("dp", "axial", None, None), P("dp")) + (P(),) * 8,
        out_specs=(P("dp", "axial", None, None),) + (P(),) * 8,
        check_vma=False,
    )
```

```python
import functools
import math

import jax
import jax.numpy as jnp
from jax import lax
from jax.experimental import pallas as pl
from jax.experimental.pallas import tpu as pltpu
from jax.sharding import PartitionSpec as P

EPSILON = 1e-05
MESH = pl.DeviceIdType.MESH
F32, BF16 = jnp.float32, jnp.bfloat16
PARTS = 32
DEPTH = 16
ROWS, TOK, C = 8, 256, 128
CHUNKS = 2
W = TOK // CHUNKS
BLOCKS = ROWS * CHUNKS
CELLS = ROWS * TOK
PIECE = 16
EARLY, LATE = 256, 128


def dot(a, b, ca=1, cb=0):
    return lax.dot_general(a, b, (((ca,), (cb,)), ((), ())), preferred_element_type=F32)


def sigmoid(v):
    return 0.5 * jnp.tanh(0.5 * v) + 0.5


def center(v):
    c = v - jnp.mean(v, axis=0, keepdims=True)
    rs = lax.rsqrt(jnp.mean(c * c, axis=0, keepdims=True) + EPSILON)
    return c * rs, rs


def center_back(grad, hat, rs):
    return rs * (
        grad
        - jnp.mean(grad, axis=0, keepdims=True)
        - hat * jnp.mean(grad * hat, axis=0, keepdims=True)
    )


FAR = (10, 6, 9, 11, 14, 2, 5, 7, 8, 13, 15, 1, 3, 4, 12)


def each_partner(me, act):
    x, y, c = lax.div(me, 8), lax.rem(lax.div(me, 2), 4), lax.rem(me, 2)

    def chip(_, codes):
        code = lax.rem(codes, 16)
        there = lax.rem(x + lax.div(code, 4), 4) * 8 + lax.rem(y + lax.rem(code, 4), 4) * 2
        act(there)
        act(there + 1)
        return lax.div(codes, 16)

    for part in (FAR[:5], FAR[5:10], FAR[10:]):
        codes = sum(code * 16**k for k, code in enumerate(part))
        lax.fori_loop(0, len(part), chip, jnp.int32(codes))
    act(me + 1 - 2 * c)


def kernel(
    len_ref, pair_hbm, cot_hbm, n1_hbm, p1_hbm, g1_hbm, f1_hbm, n2_hbm, p2_hbm, g2_hbm, f2_hbm,
    out_hbm, early_out, late_out,
    pair_ref, cot_ref, n_in, p_in, g_in, f_in, out_ref,
    gnb, ggb, pjt, pj, fnt, fw, xt, ct, xh, rsx, st, nrm, gm, fnn, gp, ih, rsi, prod,
    tmp, s2, r2, s1, r1, t1, u1, t2, u2, tri, es, er, ezs, ezr, ecs, ecr, ls, lr, lzs, lzr, lcs, lcr,
    share, ssem, rsem, isem, osem,
):
    me = lax.axis_index("axial")
    depth_me = lax.axis_index("dp")
    length = len_ref[0]

    barrier = pltpu.get_barrier_semaphore()

    def hello(t):
        pl.semaphore_signal(barrier, inc=1, device_id={"axial": t}, device_id_type=MESH)

    def hello_z(s, _):
        pl.semaphore_signal(
            barrier, inc=1, device_id={"dp": (depth_me + s) % DEPTH}, device_id_type=MESH
        )
        return 0

    lax.fori_loop(1, DEPTH, hello_z, 0)
    each_partner(me, hello)

    loads = [(pair_hbm, pair_ref), (cot_hbm, cot_ref)]
    for u, group in enumerate(
        ((n1_hbm, p1_hbm, g1_hbm, f1_hbm), (n2_hbm, p2_hbm, g2_hbm, f2_hbm))
    ):
        loads += [(h, v.at[u]) for h, v in zip(group, (n_in, p_in, g_in, f_in))]
    loads = [pltpu.make_async_copy(h, v, isem.at[i]) for i, (h, v) in enumerate(loads)]
    for i in (2, 3, 0, 4, 5, 6, 7, 8, 9, 1):
        loads[i].start()

    def weights(u):
        for k in range(4):
            loads[2 + 4 * u + k].wait()
        for vec, wide in ((n_in, gnb), (g_in, ggb)):
            wide[u] = jnp.broadcast_to(vec[u], (C, C)).T
        pj[u] = p_in[u].astype(BF16)
        pjt[u] = p_in[u].T.astype(BF16)
        fw[u] = f_in[u].astype(BF16)
        fnt[u] = f_in[u].T.astype(BF16)

    weights(0)
    loads[0].wait()

    def send(src, dst, k):
        dst[me] = src[me]

        def go(t):
            pltpu.make_async_remote_copy(
                src_ref=src.at[t], dst_ref=dst.at[me], send_sem=ssem.at[k], recv_sem=rsem.at[k],
                device_id={"axial": t}, device_id_type=MESH,
            ).start()

        each_partner(me, go)

    def arrived(src, dst, k):
        part = pl.ds(0, PARTS - 1)
        pltpu.make_async_remote_copy(
            src_ref=src.at[part], dst_ref=dst.at[part], send_sem=ssem.at[k], recv_sem=rsem.at[k],
            device_id={"axial": lax.rem(me + 1, PARTS)}, device_id_type=MESH,
        ).wait()

    def rows(body):
        lax.fori_loop(0, ROWS, lambda r, _: (body(r), 0)[1], 0, unroll=4)

    def alive(q, r):
        col = lax.broadcasted_iota(jnp.int32, (1, W), 1) + q * W
        row = jnp.zeros((1, W), jnp.int32) + (me * ROWS + r)
        return jnp.where(jnp.maximum(col, row) < length, 1.0, 0.0)

    def cut(q, r):
        return pl.ds(pl.multiple_of((q * ROWS + r) * W, W), W)

    def strided(r):
        return pl.ds(r, C, stride=ROWS)

    def entry(u, q, r, x):
        b = q * ROWS + r
        hat, rs = center(x)
        xh[u, b] = hat
        rsx[u, b] = rs
        normed = (hat * gnb[u]).astype(BF16)
        nrm[u, :, cut(q, r)] = normed
        mask = alive(q, r)
        for side in range(2):
            value = dot(pjt[u, side * C : (side + 1) * C, :], normed)
            sig = sigmoid(dot(pjt[u, (2 + side) * C : (3 + side) * C, :], normed))
            st[u, b, side * C : (side + 1) * C, :] = value
            st[u, b, (2 + side) * C : (3 + side) * C, :] = sig
            tmp[side, strided(r), :] = value * sig * mask
        st[u, b, 4 * C :, :] = sigmoid(dot(pjt[u, 4 * C :, :], normed))

    def leave(u, q, r):
        b = q * ROWS + r
        hat, rs = center(tmp[0, strided(r), :])
        ih[u, b] = hat
        rsi[u, b] = rs
        normed = (hat * ggb[u]).astype(BF16)
        fnn[u, :, cut(q, r)] = normed
        product = dot(fnt[u], normed)
        prod[u, b] = product
        return product

    def leave_back(u, q, r, grad):
        b = q * ROWS + r
        gate = st[u, b, 4 * C :, :]
        grad_product = (grad * gate).astype(BF16)
        gp[u, :, cut(q, r)] = grad_product
        gm[u, 4 * C :, cut(q, r)] = (grad * prod[u, b] * gate * (1.0 - gate)).astype(BF16)
        grad_normed = dot(fw[u], grad_product)
        hat = ih[u, b]
        tmp[0, strided(r), :] = center_back(grad_normed * ggb[u], hat, rsi[u, b])

    def gating_back(u, q, r):
        b = q * ROWS + r
        mask = alive(q, r)
        for side in range(2):
            grad = tmp[side, strided(r), :] * mask
            value = st[u, b, side * C : (side + 1) * C, :]
            sig = st[u, b, (2 + side) * C : (3 + side) * C, :]
            through = grad * sig
            gm[u, side * C : (side + 1) * C, cut(q, r)] = through.astype(BF16)
            gm[u, (2 + side) * C : (3 + side) * C, cut(q, r)] = (
                through * value * (1.0 - sig)
            ).astype(BF16)

    def entry_back(u, q, r):
        b = q * ROWS + r
        grad_normed = dot(pj[u], gm[u, :, cut(q, r)])
        hat = xh[u, b]
        return center_back(grad_normed * gnb[u], hat, rsx[u, b])

    def pack(dst, q, sides):
        def one(d, _):
            for p in range(2):
                for side in range(sides):
                    dst[p, d, q, side * 16 : (side + 1) * 16, :] = tmp[
                        side, pl.ds(pl.multiple_of(d * 32 + p * 16, 16), 16), :
                    ].astype(BF16)
            return 0

        lax.fori_loop(0, PARTS, one, 0, unroll=4)

    def unpack(src, q, sides):
        def one(d, _):
            for p in range(2):
                for side in range(sides):
                    tmp[side, pl.ds(pl.multiple_of(d * 32 + p * 16, 16), 16), :] = src[
                        q, d, p, side * 16 : (side + 1) * 16, :
                    ].astype(F32)
            return 0

        lax.fori_loop(0, PARTS, one, 0, unroll=4)

    def part(ref, i):
        return ref.at[1] if i == 2 else ref.at[0, :, i]

    def send_chunk(src, dst, k, chunk):
        for i in ((0,), (1, 2))[chunk]:
            send(part(src, i), part(dst, i), 3 * k + i)

    def arrived_part(src, dst, k, i):
        arrived(part(src, i), part(dst, i), 3 * k + i)

    def arrived_half(src, dst, k, half):
        for i in ((0, 1), (2,))[half]:
            arrived_part(src, dst, k, i)

    def channels(ref, side, p, q, to):
        block = ref[p, :, q, 16 * side : 16 * side + 16, :].astype(F32)
        block = block.reshape(PARTS, 2, ROWS, W)
        for e in range(2):
            to[2 * p + e, :, q * W : (q + 1) * W] = block[:, e].reshape(TOK, W).astype(BF16)

    def put(dst, side, p, both):
        both = jnp.concatenate([m.reshape(PARTS, ROWS, TOK) for m in both], axis=1).astype(BF16)
        for q in range(CHUNKS):
            dst[q, :, p, 16 * side : 16 * side + 16, :] = both[:, :, q * W : (q + 1) * W]

    for q in range(CHUNKS):

        def first(r):
            x = pair_ref[r, q * W : (q + 1) * W, :].astype(F32).T
            xt[q * ROWS + r] = x
            entry(0, q, r, x)

        rows(first)
        pack(s2.at[0], q, 2)
        if q == 0:
            pl.semaphore_wait(barrier, PARTS - 1 + DEPTH - 1)
        send_chunk(s2.at[0], r2.at[0], 0, q)

    weights(1)
    loads[1].wait()

    for q in range(CHUNKS):

        def turn(r):
            ct[q * ROWS + r] = cot_ref[r, q * W : (q + 1) * W, :].astype(F32).T

        rows(turn)

    def forward_triangle(u, k):
        src, dst = (s2.at[u], r2.at[u]), (t1.at[u], u1.at[u])
        for p in range(2):
            for q in range(CHUNKS):
                if (p, q) != (1, 1):
                    arrived_part(*src, k - 1, 2 * p + q)
                for side in range(2):
                    channels(src[1], side, p, q, tri.at[u, side])
            both = [
                dot(tri[u, 0, 2 * p + e], tri[u, 1, 2 * p + e], 1 - u, 1 - u) for e in range(2)
            ]
            put(dst[0], 0, p, both)
            send_chunk(*dst, k, p)

    def backward_triangle(u, k):
        src, dst = (s1.at[u], r1.at[u]), (t2.at[u], u2.at[u])
        for p in range(2):
            for q in range(CHUNKS):
                if (p, q) != (1, 1):
                    arrived_part(*src, k - 1, 2 * p + q)
                channels(src[1], 0, p, q, tri.at[2, 0])
            grad = [tri[2, 0, 2 * p + e] for e in range(2)]
            left = [tri[u, 0, 2 * p + e] for e in range(2)]
            right = [tri[u, 1, 2 * p + e] for e in range(2)]
            if u == 0:
                grad_left = [dot(grad[e], right[e]) for e in range(2)]
                grad_right = [dot(grad[e], left[e], 0, 0) for e in range(2)]
            else:
                grad_left = [dot(right[e], grad[e], 1, 1) for e in range(2)]
                grad_right = [dot(left[e], grad[e]) for e in range(2)]
            put(dst[0], 0, p, grad_left)
            put(dst[0], 1, p, grad_right)
            send_chunk(*dst, k, p)

    forward_triangle(0, 1)

    for q in range(CHUNKS):
        arrived_half(t1.at[0], u1.at[0], 1, q)
        unpack(u1.at[0], q, 1)

        def second(r):
            b = q * ROWS + r
            product = leave(0, q, r)
            middle = (xt[b] + product * st[0, b, 4 * C :, :]).astype(BF16).astype(F32)
            entry(1, q, r, middle)

        rows(second)
        pack(s2.at[1], q, 2)
        send_chunk(s2.at[1], r2.at[1], 2, q)

    forward_triangle(1, 3)

    for q in range(CHUNKS):
        arrived_half(t1.at[1], u1.at[1], 3, q)
        unpack(u1.at[1], q, 1)

        def third(r):
            leave(1, q, r)
            leave_back(1, q, r, ct[q * ROWS + r])

        rows(third)
        pack(s1.at[1], q, 1)
        send_chunk(s1.at[1], r1.at[1], 4, q)

    backward_triangle(1, 5)

    for q in range(CHUNKS):
        arrived_half(t2.at[1], u2.at[1], 5, q)
        unpack(u2.at[1], q, 2)

        def fourth(r):
            b = q * ROWS + r
            gating_back(1, q, r)
            grad = ct[b] + entry_back(1, q, r)
            ct[b] = grad
            leave_back(0, q, r, grad)

        rows(fourth)
        pack(s1.at[0], q, 1)
        send_chunk(s1.at[0], r1.at[0], 6, q)

    last = 8 * 3

    def pieces(to, grads):
        wide = grads.shape[1] // 4
        for d in range(PARTS):
            here = grads[d // 4 * PIECE : (d // 4 + 1) * PIECE, d % 4 * wide : (d % 4 + 1) * wide]
            to[d] = here.astype(BF16)

    def total(ref):
        rest = range(1, ref.shape[0])
        return functools.reduce(lambda a, d: a + ref[d].astype(F32), rest, ref[0].astype(F32))

    def send_z(src, dst, k):
        dst[depth_me] = src[...]

        def go(s, _):
            pltpu.make_async_remote_copy(
                src_ref=src, dst_ref=dst.at[depth_me], send_sem=ssem.at[k], recv_sem=rsem.at[k],
                device_id={"dp": lax.rem(depth_me + s, DEPTH)}, device_id_type=MESH,
            ).start()
            return 0

        lax.fori_loop(1, DEPTH, go, 0)

    def arrived_z(dst, k):
        part = pl.ds(0, DEPTH - 1)
        pltpu.make_async_remote_copy(
            src_ref=dst.at[part], dst_ref=dst.at[part], send_sem=ssem.at[k], recv_sem=rsem.at[k],
            device_id={"dp": lax.rem(depth_me + 1, DEPTH)}, device_id_type=MESH,
        ).wait()

    def send_all(src, dst, k):
        dst[me] = src[...]

        def go(t):
            pltpu.make_async_remote_copy(
                src_ref=src, dst_ref=dst.at[me], send_sem=ssem.at[k], recv_sem=rsem.at[k],
                device_id={"axial": t}, device_id_type=MESH,
            ).start()

        each_partner(me, go)

    early = [
        dot(nrm[1], gm[1], 1, 1),
        dot(fnn[1], gp[1], 1, 1),
        dot(nrm[0], gm[0, 4 * C :, :], 1, 1),
        dot(fnn[0], gp[0], 1, 1),
    ]
    pieces(es, jnp.concatenate(early, axis=1))
    send(es, er, last)

    backward_triangle(0, 7)

    arrived(es, er, last)
    ezs[...] = total(er).astype(BF16)
    send_z(ezs, ezr, last + 1)

    def store(q):
        here = (slice(None), pl.ds(q * W, W))
        return pltpu.make_async_copy(out_ref.at[here], out_hbm.at[here], osem.at[q])

    def fifth(q, r):
        grad = ct[q * ROWS + r] + entry_back(0, q, r)
        out_ref[r, q * W : (q + 1) * W, :] = grad.T

    for q in range(CHUNKS):
        arrived_half(t2.at[0], u2.at[0], 7, q)
        unpack(u2.at[0], q, 2)
        rows(functools.partial(gating_back, 0, q))
        if q == 0:
            rows(functools.partial(fifth, q))
            store(q).start()
            cells = ROWS * W
            share[...] = dot(nrm[0, :, :cells], gm[0, : 4 * C, :cells], 1, 1)

    scale = 1.0 / math.sqrt(DEPTH * TOK * TOK)
    pieces(ls, share[...] + dot(nrm[0, :, cells:], gm[0, : 4 * C, cells:], 1, 1))
    send(ls, lr, last + 3)
    rows(functools.partial(fifth, 1))
    store(1).start()
    arrived_z(ezr, last + 1)
    ecs[...] = (total(ezr) * scale).astype(BF16)
    arrived(ls, lr, last + 3)
    lzs[...] = total(lr).astype(BF16)
    send_z(lzs, lzr, last + 4)
    send_all(ecs, ecr, last + 2)
    arrived_z(lzr, last + 4)
    lcs[...] = (total(lzr) * scale).astype(BF16)
    send_all(lcs, lcr, last + 5)
    arrived(ecr, ecr, last + 2)
    early_out[...] = ecr[...]
    for q in range(CHUNKS):
        store(q).wait()
    arrived(lcr, lcr, last + 5)
    late_out[...] = lcr[...]


def finish(
    big, early, late, n1, p1, g1, f1, n2, p2, g2, f2, out, on1, op1, og1, of1, on2, op2, og2, of2
):
    out[...] = big[...]
    for i in range(C // PIECE):
        here = slice(i * PIECE, (i + 1) * PIECE)
        blocks = [early[4 * i + j].astype(F32) for j in range(4)]
        for j in range(4):
            op1[here, j * LATE : (j + 1) * LATE] = late[4 * i + j].astype(F32)
        op1[here, 4 * C :] = blocks[3][:, :C]
        of1[here, :] = blocks[3][:, C:]
        op2[here, : 2 * C] = blocks[0]
        op2[here, 2 * C : 4 * C] = blocks[1]
        op2[here, 4 * C :] = blocks[2][:, :C]
        of2[here, :] = blocks[2][:, C:]

    def gain(to, by, weight, grad):
        both = weight[...].astype(BF16).astype(F32) * grad[...]
        both = sum(both[:, j * C : (j + 1) * C] for j in range(both.shape[1] // C))
        to[...] = jnp.sum(both.T, axis=0, keepdims=True) / by[...]

    gain(on1, n1, p1, op1)
    gain(og1, g1, f1, of1)
    gain(on2, n2, p2, op2)
    gain(og2, g2, f2, of2)


def body(pair, cotangent, lengths, *weights):
    weights = [w.reshape(1, C) if w.ndim == 1 else w for w in weights]
    vmem = pl.BlockSpec(memory_space=pltpu.VMEM)
    sums = [jax.ShapeDtypeStruct(w.shape, F32) for w in weights]
    hbm = pl.BlockSpec(memory_space=pl.ANY)
    parts = pl.pallas_call(
        kernel,
        out_shape=[
            jax.ShapeDtypeStruct((ROWS, TOK, C), F32),
            jax.ShapeDtypeStruct((PARTS, PIECE, EARLY), BF16),
            jax.ShapeDtypeStruct((PARTS, PIECE, LATE), BF16),
        ],
        in_specs=[pl.BlockSpec(memory_space=pltpu.SMEM)] + [hbm] * 10,
        out_specs=[hbm, vmem, vmem],
        scratch_shapes=[
            pltpu.VMEM((ROWS, TOK, C), BF16),
            pltpu.VMEM((ROWS, TOK, C), BF16),
            pltpu.VMEM((2, 1, C), F32),
            pltpu.VMEM((2, C, 5 * C), F32),
            pltpu.VMEM((2, 1, C), F32),
            pltpu.VMEM((2, C, C), F32),
            pltpu.VMEM((ROWS, TOK, C), F32),
            pltpu.VMEM((2, C, W), F32),
            pltpu.VMEM((2, C, W), F32),
            pltpu.VMEM((2, 5 * C, C), BF16),
            pltpu.VMEM((2, C, 5 * C), BF16),
            pltpu.VMEM((2, C, C), BF16),
            pltpu.VMEM((2, C, C), BF16),
            pltpu.VMEM((BLOCKS, C, W), F32),
            pltpu.VMEM((BLOCKS, C, W), F32),
            pltpu.VMEM((2, BLOCKS, C, W), F32),
            pltpu.VMEM((2, BLOCKS, 1, W), F32),
            pltpu.VMEM((2, BLOCKS, 5 * C, W), F32),
            pltpu.VMEM((2, C, CELLS), BF16),
            pltpu.VMEM((2, 5 * C, CELLS), BF16),
            pltpu.VMEM((2, C, CELLS), BF16),
            pltpu.VMEM((2, C, CELLS), BF16),
            pltpu.VMEM((2, BLOCKS, C, W), F32),
            pltpu.VMEM((2, BLOCKS, 1, W), F32),
            pltpu.VMEM((2, BLOCKS, C, W), F32),
            pltpu.VMEM((2, C * ROWS, W), F32),
        ]
        + [
            pltpu.VMEM((2, 2, PARTS, 2, 16 * sides, W), BF16)
            for sides in (2, 2, 1, 1, 1, 1, 2, 2)
        ]
        + [
            pltpu.VMEM((3, 2, 4, TOK, TOK), BF16),
        ]
        + [
            pltpu.VMEM(shape + (PIECE, wide), BF16)
            for wide in (EARLY, LATE)
            for shape in ((PARTS,), (PARTS,), (), (DEPTH,), (), (PARTS,))
        ]
        + [
            pltpu.VMEM((C, 4 * C), F32),
            pltpu.SemaphoreType.DMA((8 * 3 + 6,)),
            pltpu.SemaphoreType.DMA((8 * 3 + 6,)),
            pltpu.SemaphoreType.DMA((10,)),
            pltpu.SemaphoreType.DMA((CHUNKS,)),
        ],
        compiler_params=pltpu.CompilerParams(
            collective_id=0, has_side_effects=True, vmem_limit_bytes=60 << 20
        ),
    )(lengths, pair[0], cotangent[0], *weights)
    outs = pl.pallas_call(
        finish,
        out_shape=[jax.ShapeDtypeStruct((ROWS, TOK, C), F32)] + sums,
        in_specs=[vmem] * 11,
        out_specs=[vmem] * 9,
        compiler_params=pltpu.CompilerParams(vmem_limit_bytes=60 << 20),
    )(*parts, *weights)
    grads = [o.reshape(C) if o.shape[0] == 1 else o for o in outs[1:]]
    return (outs[0][None], *grads)


def solution(mesh):
    return jax.shard_map(
        body,
        mesh=mesh,
        in_specs=(P("dp", "axial", None, None), P("dp", "axial", None, None), P("dp")) + (P(),) * 8,
        out_specs=(P("dp", "axial", None, None),) + (P(),) * 8,
        check_vma=False,
    )
```

```python
import functools
import math

import jax
import jax.numpy as jnp
from jax import lax
from jax.experimental import pallas as pl
from jax.experimental.pallas import tpu as pltpu
from jax.sharding import PartitionSpec as P

EPSILON = 1e-05
MESH = pl.DeviceIdType.MESH
F32, BF16 = jnp.float32, jnp.bfloat16
PARTS = 32
DEPTH = 16
ROWS, TOK, C = 8, 256, 128
CHUNKS = 2
W = TOK // CHUNKS
BLOCKS = ROWS * CHUNKS
CELLS = ROWS * TOK
PIECE = 16
EARLY, LATE = 256, 128


def dot(a, b, ca=1, cb=0):
    return lax.dot_general(a, b, (((ca,), (cb,)), ((), ())), preferred_element_type=F32)


def sigmoid(v):
    return 0.5 * jnp.tanh(0.5 * v) + 0.5


def center(v):
    c = v - jnp.mean(v, axis=0, keepdims=True)
    rs = lax.rsqrt(jnp.mean(c * c, axis=0, keepdims=True) + EPSILON)
    return c * rs, rs


def center_back(grad, hat, rs):
    return rs * (
        grad
        - jnp.mean(grad, axis=0, keepdims=True)
        - hat * jnp.mean(grad * hat, axis=0, keepdims=True)
    )


FAR = (10, 6, 9, 11, 14, 2, 5, 7, 8, 13, 15, 1, 3, 4, 12)


def each_partner(me, act):
    x, y, c = lax.div(me, 8), lax.rem(lax.div(me, 2), 4), lax.rem(me, 2)

    def chip(_, codes):
        code = lax.rem(codes, 16)
        there = lax.rem(x + lax.div(code, 4), 4) * 8 + lax.rem(y + lax.rem(code, 4), 4) * 2
        act(there)
        act(there + 1)
        return lax.div(codes, 16)

    for part in (FAR[:5], FAR[5:10], FAR[10:]):
        codes = sum(code * 16**k for k, code in enumerate(part))
        lax.fori_loop(0, len(part), chip, jnp.int32(codes))
    act(me + 1 - 2 * c)


def kernel(
    len_ref, pair_hbm, cot_hbm, n1_hbm, p1_hbm, g1_hbm, f1_hbm, n2_hbm, p2_hbm, g2_hbm, f2_hbm,
    out_hbm, early_out, late_out,
    pair_ref, cot_ref, n_in, p_in, g_in, f_in, out_ref,
    gnb, ggb, pjt, pj, fnt, fw, xt, ct, xh, rsx, st, nrm, gm, fnn, gp, ih, rsi, prod,
    tmp, s2, r2, s1, r1, t1, u1, t2, u2, tri, es, er, ezs, ezr, ecs, ecr, ls, lr, lzs, lzr, lcs, lcr,
    share, ssem, rsem, isem, osem,
):
    me = lax.axis_index("axial")
    depth_me = lax.axis_index("dp")
    length = len_ref[0]

    barrier = pltpu.get_barrier_semaphore()

    def hello(t):
        pl.semaphore_signal(barrier, inc=1, device_id={"axial": t}, device_id_type=MESH)

    def hello_z(s, _):
        pl.semaphore_signal(
            barrier, inc=1, device_id={"dp": (depth_me + s) % DEPTH}, device_id_type=MESH
        )
        return 0

    lax.fori_loop(1, DEPTH, hello_z, 0)
    each_partner(me, hello)

    loads = [(pair_hbm, pair_ref), (cot_hbm, cot_ref)]
    for u, group in enumerate(
        ((n1_hbm, p1_hbm, g1_hbm, f1_hbm), (n2_hbm, p2_hbm, g2_hbm, f2_hbm))
    ):
        loads += [(h, v.at[u]) for h, v in zip(group, (n_in, p_in, g_in, f_in))]
    loads = [pltpu.make_async_copy(h, v, isem.at[i]) for i, (h, v) in enumerate(loads)]
    for i in (2, 3, 0, 4, 5, 6, 7, 8, 9, 1):
        loads[i].start()

    def weights(u):
        for k in range(4):
            loads[2 + 4 * u + k].wait()
        for vec, wide in ((n_in, gnb), (g_in, ggb)):
            wide[u] = jnp.broadcast_to(vec[u], (C, C)).T
        pj[u] = p_in[u].astype(BF16)
        pjt[u] = p_in[u].T.astype(BF16)
        fw[u] = f_in[u].astype(BF16)
        fnt[u] = f_in[u].T.astype(BF16)

    weights(0)
    loads[0].wait()

    def send(src, dst, k):
        dst[me] = src[me]

        def go(t):
            pltpu.make_async_remote_copy(
                src_ref=src.at[t], dst_ref=dst.at[me], send_sem=ssem.at[k], recv_sem=rsem.at[k],
                device_id={"axial": t}, device_id_type=MESH,
            ).start()

        each_partner(me, go)

    def arrived(src, dst, k):
        part = pl.ds(0, PARTS - 1)
        pltpu.make_async_remote_copy(
            src_ref=src.at[part], dst_ref=dst.at[part], send_sem=ssem.at[k], recv_sem=rsem.at[k],
            device_id={"axial": lax.rem(me + 1, PARTS)}, device_id_type=MESH,
        ).wait()

    def rows(body):
        lax.fori_loop(0, ROWS, lambda r, _: (body(r), 0)[1], 0, unroll=4)

    def alive(q, r):
        col = lax.broadcasted_iota(jnp.int32, (1, W), 1) + q * W
        row = jnp.zeros((1, W), jnp.int32) + (me * ROWS + r)
        return jnp.where(jnp.maximum(col, row) < length, 1.0, 0.0)

    def cut(q, r):
        return pl.ds(pl.multiple_of((q * ROWS + r) * W, W), W)

    def strided(r):
        return pl.ds(r, C, stride=ROWS)

    def entry(u, q, r, x):
        b = q * ROWS + r
        hat, rs = center(x)
        xh[u, b] = hat
        rsx[u, b] = rs
        normed = (hat * gnb[u]).astype(BF16)
        nrm[u, :, cut(q, r)] = normed
        mask = alive(q, r)
        for side in range(2):
            value = dot(pjt[u, side * C : (side + 1) * C, :], normed)
            sig = sigmoid(dot(pjt[u, (2 + side) * C : (3 + side) * C, :], normed))
            st[u, b, side * C : (side + 1) * C, :] = value
            st[u, b, (2 + side) * C : (3 + side) * C, :] = sig
            tmp[side, strided(r), :] = value * sig * mask

    def output_gate(u, q, r):
        normed = nrm[u, :, cut(q, r)]
        st[u, q * ROWS + r, 4 * C :, :] = sigmoid(dot(pjt[u, 4 * C :, :], normed))

    def leave(u, q, r):
        b = q * ROWS + r
        hat, rs = center(tmp[0, strided(r), :])
        ih[u, b] = hat
        rsi[u, b] = rs
        normed = (hat * ggb[u]).astype(BF16)
        fnn[u, :, cut(q, r)] = normed
        product = dot(fnt[u], normed)
        prod[u, b] = product
        return product

    def leave_back(u, q, r, grad):
        b = q * ROWS + r
        gate = st[u, b, 4 * C :, :]
        grad_product = (grad * gate).astype(BF16)
        gp[u, :, cut(q, r)] = grad_product
        gm[u, 4 * C :, cut(q, r)] = (grad * prod[u, b] * gate * (1.0 - gate)).astype(BF16)
        grad_normed = dot(fw[u], grad_product)
        hat = ih[u, b]
        tmp[0, strided(r), :] = center_back(grad_normed * ggb[u], hat, rsi[u, b])

    def gating_back(u, q, r):
        b = q * ROWS + r
        mask = alive(q, r)
        for side in range(2):
            grad = tmp[side, strided(r), :] * mask
            value = st[u, b, side * C : (side + 1) * C, :]
            sig = st[u, b, (2 + side) * C : (3 + side) * C, :]
            through = grad * sig
            gm[u, side * C : (side + 1) * C, cut(q, r)] = through.astype(BF16)
            gm[u, (2 + side) * C : (3 + side) * C, cut(q, r)] = (
                through * value * (1.0 - sig)
            ).astype(BF16)

    def entry_back(u, q, r):
        b = q * ROWS + r
        grad_normed = dot(pj[u], gm[u, :, cut(q, r)])
        hat = xh[u, b]
        return center_back(grad_normed * gnb[u], hat, rsx[u, b])

    def pack(dst, q, sides):
        def one(d, _):
            for p in range(2):
                for side in range(sides):
                    dst[p, d, q, side * 16 : (side + 1) * 16, :] = tmp[
                        side, pl.ds(pl.multiple_of(d * 32 + p * 16, 16), 16), :
                    ].astype(BF16)
            return 0

        lax.fori_loop(0, PARTS, one, 0, unroll=4)

    def unpack(src, q, sides):
        def one(d, _):
            for p in range(2):
                for side in range(sides):
                    tmp[side, pl.ds(pl.multiple_of(d * 32 + p * 16, 16), 16), :] = src[
                        q, d, p, side * 16 : (side + 1) * 16, :
                    ].astype(F32)
            return 0

        lax.fori_loop(0, PARTS, one, 0, unroll=4)

    def part(ref, i):
        return ref.at[1] if i == 2 else ref.at[0, :, i]

    def send_chunk(src, dst, k, chunk):
        for i in ((0,), (1, 2))[chunk]:
            send(part(src, i), part(dst, i), 3 * k + i)

    def arrived_part(src, dst, k, i):
        arrived(part(src, i), part(dst, i), 3 * k + i)

    def arrived_half(src, dst, k, half):
        for i in ((0, 1), (2,))[half]:
            arrived_part(src, dst, k, i)

    def channels(ref, side, p, q, to):
        block = ref[p, :, q, 16 * side : 16 * side + 16, :].astype(F32)
        block = block.reshape(PARTS, 2, ROWS, W)
        for e in range(2):
            to[2 * p + e, :, q * W : (q + 1) * W] = block[:, e].reshape(TOK, W).astype(BF16)

    def put(dst, side, p, both):
        both = jnp.concatenate([m.reshape(PARTS, ROWS, TOK) for m in both], axis=1).astype(BF16)
        for q in range(CHUNKS):
            dst[q, :, p, 16 * side : 16 * side + 16, :] = both[:, :, q * W : (q + 1) * W]

    for q in range(CHUNKS):

        def first(r):
            x = pair_ref[r, q * W : (q + 1) * W, :].astype(F32).T
            xt[q * ROWS + r] = x
            entry(0, q, r, x)

        rows(first)
        pack(s2.at[0], q, 2)
        if q == 0:
            pl.semaphore_wait(barrier, PARTS - 1 + DEPTH - 1)
        send_chunk(s2.at[0], r2.at[0], 0, q)

    weights(1)
    loads[1].wait()

    for q in range(CHUNKS):

        def turn(r):
            ct[q * ROWS + r] = cot_ref[r, q * W : (q + 1) * W, :].astype(F32).T
            output_gate(0, q, r)

        rows(turn)

    def forward_triangle(u, k):
        src, dst = (s2.at[u], r2.at[u]), (t1.at[u], u1.at[u])
        for p in range(2):
            for q in range(CHUNKS):
                if (p, q) != (1, 1):
                    arrived_part(*src, k - 1, 2 * p + q)
                for side in range(2):
                    channels(src[1], side, p, q, tri.at[u, side])
            both = [
                dot(tri[u, 0, 2 * p + e], tri[u, 1, 2 * p + e], 1 - u, 1 - u) for e in range(2)
            ]
            put(dst[0], 0, p, both)
            send_chunk(*dst, k, p)

    def backward_triangle(u, k):
        src, dst = (s1.at[u], r1.at[u]), (t2.at[u], u2.at[u])
        for p in range(2):
            for q in range(CHUNKS):
                if (p, q) != (1, 1):
                    arrived_part(*src, k - 1, 2 * p + q)
                channels(src[1], 0, p, q, tri.at[2, 0])
            grad = [tri[2, 0, 2 * p + e] for e in range(2)]
            left = [tri[u, 0, 2 * p + e] for e in range(2)]
            right = [tri[u, 1, 2 * p + e] for e in range(2)]
            if u == 0:
                grad_left = [dot(grad[e], right[e]) for e in range(2)]
                grad_right = [dot(grad[e], left[e], 0, 0) for e in range(2)]
            else:
                grad_left = [dot(right[e], grad[e], 1, 1) for e in range(2)]
                grad_right = [dot(left[e], grad[e]) for e in range(2)]
            put(dst[0], 0, p, grad_left)
            put(dst[0], 1, p, grad_right)
            send_chunk(*dst, k, p)

    forward_triangle(0, 1)

    for q in range(CHUNKS):
        arrived_half(t1.at[0], u1.at[0], 1, q)
        unpack(u1.at[0], q, 1)

        def second(r):
            b = q * ROWS + r
            product = leave(0, q, r)
            middle = (xt[b] + product * st[0, b, 4 * C :, :]).astype(BF16).astype(F32)
            entry(1, q, r, middle)

        rows(second)
        pack(s2.at[1], q, 2)
        send_chunk(s2.at[1], r2.at[1], 2, q)

    for q in range(CHUNKS):
        rows(functools.partial(output_gate, 1, q))

    forward_triangle(1, 3)

    for q in range(CHUNKS):
        arrived_half(t1.at[1], u1.at[1], 3, q)
        unpack(u1.at[1], q, 1)

        def third(r):
            leave(1, q, r)
            leave_back(1, q, r, ct[q * ROWS + r])

        rows(third)
        pack(s1.at[1], q, 1)
        send_chunk(s1.at[1], r1.at[1], 4, q)

    backward_triangle(1, 5)

    for q in range(CHUNKS):
        arrived_half(t2.at[1], u2.at[1], 5, q)
        unpack(u2.at[1], q, 2)

        def fourth(r):
            b = q * ROWS + r
            gating_back(1, q, r)
            grad = ct[b] + entry_back(1, q, r)
            ct[b] = grad
            leave_back(0, q, r, grad)

        rows(fourth)
        pack(s1.at[0], q, 1)
        send_chunk(s1.at[0], r1.at[0], 6, q)

    last = 8 * 3

    def pieces(to, grads):
        wide = grads.shape[1] // 4
        for d in range(PARTS):
            here = grads[d // 4 * PIECE : (d // 4 + 1) * PIECE, d % 4 * wide : (d % 4 + 1) * wide]
            to[d] = here.astype(BF16)

    def total(ref):
        rest = range(1, ref.shape[0])
        return functools.reduce(lambda a, d: a + ref[d].astype(F32), rest, ref[0].astype(F32))

    def send_z(src, dst, k):
        dst[depth_me] = src[...]

        def go(s, _):
            pltpu.make_async_remote_copy(
                src_ref=src, dst_ref=dst.at[depth_me], send_sem=ssem.at[k], recv_sem=rsem.at[k],
                device_id={"dp": lax.rem(depth_me + s, DEPTH)}, device_id_type=MESH,
            ).start()
            return 0

        lax.fori_loop(1, DEPTH, go, 0)

    def arrived_z(dst, k):
        part = pl.ds(0, DEPTH - 1)
        pltpu.make_async_remote_copy(
            src_ref=dst.at[part], dst_ref=dst.at[part], send_sem=ssem.at[k], recv_sem=rsem.at[k],
            device_id={"dp": lax.rem(depth_me + 1, DEPTH)}, device_id_type=MESH,
        ).wait()

    def send_all(src, dst, k):
        dst[me] = src[...]

        def go(t):
            pltpu.make_async_remote_copy(
                src_ref=src, dst_ref=dst.at[me], send_sem=ssem.at[k], recv_sem=rsem.at[k],
                device_id={"axial": t}, device_id_type=MESH,
            ).start()

        each_partner(me, go)

    early = [
        dot(nrm[1], gm[1], 1, 1),
        dot(fnn[1], gp[1], 1, 1),
        dot(nrm[0], gm[0, 4 * C :, :], 1, 1),
        dot(fnn[0], gp[0], 1, 1),
    ]
    pieces(es, jnp.concatenate(early, axis=1))
    send(es, er, last)

    backward_triangle(0, 7)

    arrived(es, er, last)
    ezs[...] = total(er).astype(BF16)
    send_z(ezs, ezr, last + 1)

    def store(q):
        here = (slice(None), pl.ds(q * W, W))
        return pltpu.make_async_copy(out_ref.at[here], out_hbm.at[here], osem.at[q])

    def fifth(q, r):
        grad = ct[q * ROWS + r] + entry_back(0, q, r)
        out_ref[r, q * W : (q + 1) * W, :] = grad.T

    for q in range(CHUNKS):
        arrived_half(t2.at[0], u2.at[0], 7, q)
        unpack(u2.at[0], q, 2)
        rows(functools.partial(gating_back, 0, q))
        if q == 0:
            rows(functools.partial(fifth, q))
            store(q).start()
            cells = ROWS * W
            share[...] = dot(nrm[0, :, :cells], gm[0, : 4 * C, :cells], 1, 1)

    scale = 1.0 / math.sqrt(DEPTH * TOK * TOK)
    pieces(ls, share[...] + dot(nrm[0, :, cells:], gm[0, : 4 * C, cells:], 1, 1))
    send(ls, lr, last + 3)
    rows(functools.partial(fifth, 1))
    store(1).start()
    arrived_z(ezr, last + 1)
    ecs[...] = (total(ezr) * scale).astype(BF16)
    arrived(ls, lr, last + 3)
    lzs[...] = total(lr).astype(BF16)
    send_z(lzs, lzr, last + 4)
    send_all(ecs, ecr, last + 2)
    arrived_z(lzr, last + 4)
    lcs[...] = (total(lzr) * scale).astype(BF16)
    send_all(lcs, lcr, last + 5)
    arrived(ecr, ecr, last + 2)
    early_out[...] = ecr[...]
    for q in range(CHUNKS):
        store(q).wait()
    arrived(lcr, lcr, last + 5)
    late_out[...] = lcr[...]


def finish(
    big, early, late, n1, p1, g1, f1, n2, p2, g2, f2, out, on1, op1, og1, of1, on2, op2, og2, of2
):
    out[...] = big[...]
    for i in range(C // PIECE):
        here = slice(i * PIECE, (i + 1) * PIECE)
        blocks = [early[4 * i + j].astype(F32) for j in range(4)]
        for j in range(4):
            op1[here, j * LATE : (j + 1) * LATE] = late[4 * i + j].astype(F32)
        op1[here, 4 * C :] = blocks[3][:, :C]
        of1[here, :] = blocks[3][:, C:]
        op2[here, : 2 * C] = blocks[0]
        op2[here, 2 * C : 4 * C] = blocks[1]
        op2[here, 4 * C :] = blocks[2][:, :C]
        of2[here, :] = blocks[2][:, C:]

    def gain(to, by, weight, grad):
        both = weight[...].astype(BF16).astype(F32) * grad[...]
        both = sum(both[:, j * C : (j + 1) * C] for j in range(both.shape[1] // C))
        to[...] = jnp.sum(both.T, axis=0, keepdims=True) / by[...]

    gain(on1, n1, p1, op1)
    gain(og1, g1, f1, of1)
    gain(on2, n2, p2, op2)
    gain(og2, g2, f2, of2)


def body(pair, cotangent, lengths, *weights):
    weights = [w.reshape(1, C) if w.ndim == 1 else w for w in weights]
    vmem = pl.BlockSpec(memory_space=pltpu.VMEM)
    sums = [jax.ShapeDtypeStruct(w.shape, F32) for w in weights]
    hbm = pl.BlockSpec(memory_space=pl.ANY)
    parts = pl.pallas_call(
        kernel,
        out_shape=[
            jax.ShapeDtypeStruct((ROWS, TOK, C), F32),
            jax.ShapeDtypeStruct((PARTS, PIECE, EARLY), BF16),
            jax.ShapeDtypeStruct((PARTS, PIECE, LATE), BF16),
        ],
        in_specs=[pl.BlockSpec(memory_space=pltpu.SMEM)] + [hbm] * 10,
        out_specs=[hbm, vmem, vmem],
        scratch_shapes=[
            pltpu.VMEM((ROWS, TOK, C), BF16),
            pltpu.VMEM((ROWS, TOK, C), BF16),
            pltpu.VMEM((2, 1, C), F32),
            pltpu.VMEM((2, C, 5 * C), F32),
            pltpu.VMEM((2, 1, C), F32),
            pltpu.VMEM((2, C, C), F32),
            pltpu.VMEM((ROWS, TOK, C), F32),
            pltpu.VMEM((2, C, W), F32),
            pltpu.VMEM((2, C, W), F32),
            pltpu.VMEM((2, 5 * C, C), BF16),
            pltpu.VMEM((2, C, 5 * C), BF16),
            pltpu.VMEM((2, C, C), BF16),
            pltpu.VMEM((2, C, C), BF16),
            pltpu.VMEM((BLOCKS, C, W), F32),
            pltpu.VMEM((BLOCKS, C, W), F32),
            pltpu.VMEM((2, BLOCKS, C, W), F32),
            pltpu.VMEM((2, BLOCKS, 1, W), F32),
            pltpu.VMEM((2, BLOCKS, 5 * C, W), F32),
            pltpu.VMEM((2, C, CELLS), BF16),
            pltpu.VMEM((2, 5 * C, CELLS), BF16),
            pltpu.VMEM((2, C, CELLS), BF16),
            pltpu.VMEM((2, C, CELLS), BF16),
            pltpu.VMEM((2, BLOCKS, C, W), F32),
            pltpu.VMEM((2, BLOCKS, 1, W), F32),
            pltpu.VMEM((2, BLOCKS, C, W), F32),
            pltpu.VMEM((2, C * ROWS, W), F32),
        ]
        + [
            pltpu.VMEM((2, 2, PARTS, 2, 16 * sides, W), BF16)
            for sides in (2, 2, 1, 1, 1, 1, 2, 2)
        ]
        + [
            pltpu.VMEM((3, 2, 4, TOK, TOK), BF16),
        ]
        + [
            pltpu.VMEM(shape + (PIECE, wide), BF16)
            for wide in (EARLY, LATE)
            for shape in ((PARTS,), (PARTS,), (), (DEPTH,), (), (PARTS,))
        ]
        + [
            pltpu.VMEM((C, 4 * C), F32),
            pltpu.SemaphoreType.DMA((8 * 3 + 6,)),
            pltpu.SemaphoreType.DMA((8 * 3 + 6,)),
            pltpu.SemaphoreType.DMA((10,)),
            pltpu.SemaphoreType.DMA((CHUNKS,)),
        ],
        compiler_params=pltpu.CompilerParams(
            collective_id=0, has_side_effects=True, vmem_limit_bytes=60 << 20
        ),
    )(lengths, pair[0], cotangent[0], *weights)
    outs = pl.pallas_call(
        finish,
        out_shape=[jax.ShapeDtypeStruct((ROWS, TOK, C), F32)] + sums,
        in_specs=[vmem] * 11,
        out_specs=[vmem] * 9,
        compiler_params=pltpu.CompilerParams(vmem_limit_bytes=60 << 20),
    )(*parts, *weights)
    grads = [o.reshape(C) if o.shape[0] == 1 else o for o in outs[1:]]
    return (outs[0][None], *grads)


def solution(mesh):
    return jax.shard_map(
        body,
        mesh=mesh,
        in_specs=(P("dp", "axial", None, None), P("dp", "axial", None, None), P("dp")) + (P(),) * 8,
        out_specs=(P("dp", "axial", None, None),) + (P(),) * 8,
        check_vma=False,
    )
```
